128 devices in a mesh: seq: 32 (over y, z, core), head: 4 (over x).
Axes of the slice: x: 4, y: 4, z: 4, core: 2. Of those that a mesh axis runs over, the one named last changes fastest.
Arguments:
- queries: bfloat16 [32768, 1024], P('seq', 'head'), may hold values from -6 to 6
- keys_values: bfloat16 [32768, 128], P('seq'), may hold values from -6 to 6
- init_state: float32 [64, 2080], replicated, may hold values from -48 to 48
- out_grad: bfloat16 [32768, 1024], P('seq', 'head'), may hold values from -6 to 6
Outputs:
- attended: bfloat16 [32768, 1024], P('seq', 'head')
- query_grad: bfloat16 [32768, 1024], P('seq', 'head')
- kv_grad: float32 [32768, 128], P('seq')
- init_grad: float32 [64, 2080], P(None, 'head')
The draws below stay inside these ranges and needn't reach their ends.
All inputs are finite; a program needn't handle non-finite values.
Results may differ from the reference program's by a relative error of at most 0.0071.
Values sent between devices are 32-bit elements; how exact they have to be, the bound alone decides.
No kernel may reach another device: no remote copies, remote signals or barrier semaphores. Data moves between devices by JAX's collectives and lax.ppermute only.
A program may use at most 128 MiB of HBM per device.

```python
import jax
import jax.numpy as jnp
import numpy as np
from jax import lax

HEADS = 16
HEAD_DIM = 64
FEATURES = 2080
GROUP = 1024
TOKENS = 32768


def steps_of(rng, dims, shards, least, high):
    level, own = 1.0, jax.random.fold_in(rng, 6)
    for axis_at, blocks in shards:
        steps = jnp.exp(jax.random.uniform(jax.random.fold_in(own, axis_at), (blocks,), jnp.float32, least / len(shards), high / len(shards)))
        level = level * jnp.repeat(steps, dims[axis_at] // blocks).reshape([-1 if axis == axis_at else 1 for axis in range(len(dims))])
    return level


def bell_draw(key, dims, spread, bound, cuts=(), kind=jnp.bfloat16):
    values = spread * jax.random.normal(key, dims, jnp.float32)
    if cuts:
        values = values * steps_of(key, dims, cuts, -0.22, 0.18)
    return jnp.clip(values, -bound, bound).astype(kind)


def setup_inputs(seed: int = 0) -> dict:
    key_of = jax.random.split(jax.random.key(seed), 5)
    return {
        "queries": bell_draw(key_of[0], (TOKENS, HEADS * HEAD_DIM), 1.0, 6.0, ((0, 32), (1, 4))),
        "keys_values": bell_draw(key_of[1], (TOKENS, 2 * HEAD_DIM), 1.0, 6.0, ((0, 32),)),
        "init_state": bell_draw(key_of[2], (HEAD_DIM, FEATURES), 8.0, 48.0, (), jnp.float32),
        "out_grad": bell_draw(key_of[3], (TOKENS, HEADS * HEAD_DIM), 1.0, 6.0, ((0, 32), (1, 4))),
    }


epsilon = 1e-06

def pair_tables(width):
    left_index, right_index = np.triu_indices(width)
    factor = np.where(left_index == right_index, 1.0, np.sqrt(2.0)) / np.sqrt(width)
    return (jnp.asarray(left_index, jnp.int32), jnp.asarray(right_index, jnp.int32), jnp.asarray(factor, jnp.float32))

def product(first, second, contract):
    return lax.dot_general(first.astype(jnp.float32), second.astype(jnp.float32), (contract, ((), ())), precision=lax.Precision.HIGHEST, preferred_element_type=jnp.float32)

def features(wide, tables):
    left_index, right_index, factor = tables
    return jnp.take(wide, left_index, axis=1) * jnp.take(wide, right_index, axis=1) * factor

def feature_grad(rows_in, upstream, tables):
    _, pullback = jax.vjp(lambda inner: features(inner, tables), rows_in.astype(jnp.float32))
    return pullback(lax.optimization_barrier(upstream).astype(jnp.float32))[0]

def head_pass(query, keys, values, start_low, grad, tables):
    width = query.shape[1]
    length = query.shape[0]
    qfeat = features(query.astype(jnp.float32), tables).astype(jnp.bfloat16)
    inter = product(qfeat, start_low, ((1,), (1,)))
    logits = product(query, keys, ((1,), (1,)))
    causal = lax.broadcasted_iota(jnp.int32, (length, length), 0) >= lax.broadcasted_iota(jnp.int32, (length, length), 1)
    weights = jnp.where(causal, logits * logits / width, 0.0).astype(jnp.bfloat16)
    numer = inter + product(weights, values, ((1,), (0,)))
    scale = lax.rsqrt(lax.optimization_barrier(jnp.mean(numer * numer, axis=1, keepdims=True)) + epsilon)
    normed = numer * scale
    upstream = grad.astype(jnp.float32)
    d_numer = (scale * (upstream - normed * lax.optimization_barrier(jnp.mean(upstream * normed, axis=1, keepdims=True)))).astype(jnp.bfloat16)
    d_qfeat = product(d_numer, start_low, ((1,), (0,))).astype(jnp.bfloat16)
    d_weights = product(d_numer, values, ((1,), (1,)))
    d_logits = jnp.where(causal, d_weights * logits * (2.0 / width), 0.0).astype(jnp.bfloat16)
    query_total = feature_grad(query, d_qfeat, tables) + product(d_logits, keys, ((1,), (0,)))
    key_local = product(d_logits, query, ((0,), (0,)))
    value_local = product(weights, d_numer, ((0,), (0,)))
    state_local = product(d_numer, qfeat, ((0,), (0,)))
    return (normed.astype(jnp.bfloat16), query_total.astype(jnp.bfloat16), key_local, value_local, state_local)

def reference(queries, keys_values, init_state, out_grad):
    tables = pair_tables(HEAD_DIM)
    count = TOKENS // GROUP
    query_blocks = queries.reshape(count, GROUP, HEADS * HEAD_DIM)
    kv_blocks = keys_values.reshape(count, GROUP, 2 * HEAD_DIM)
    grad_blocks = out_grad.reshape(count, GROUP, HEADS * HEAD_DIM)

    def block_update(block):
        kfeat = features(block[:, :HEAD_DIM].astype(jnp.float32), tables).astype(jnp.bfloat16)
        return product(block[:, HEAD_DIM:], kfeat, ((0,), (0,)))
    updates = lax.map(block_update, kv_blocks)
    before = jnp.concatenate([jnp.zeros_like(updates[:1]), jnp.cumsum(updates[:-1], axis=0)], axis=0)
    starts = (init_state[None] + before).astype(jnp.bfloat16)

    def block_pass(inputs):
        query_block, kv_block, grad_block, start_low = inputs
        keys = kv_block[:, :HEAD_DIM]
        values = kv_block[:, HEAD_DIM:]
        query_heads = query_block.reshape(GROUP, HEADS, HEAD_DIM).transpose(1, 0, 2)
        grad_heads = grad_block.reshape(GROUP, HEADS, HEAD_DIM).transpose(1, 0, 2)

        def one_head(pair):
            return head_pass(pair[0], keys, values, start_low, pair[1], tables)
        normed, qgrad, key_part, value_part, state_part = lax.map(one_head, (query_heads, grad_heads))
        return (normed.transpose(1, 0, 2).reshape(GROUP, HEADS * HEAD_DIM), qgrad.transpose(1, 0, 2).reshape(GROUP, HEADS * HEAD_DIM), lax.optimization_barrier(jnp.sum(key_part, axis=0)), lax.optimization_barrier(jnp.sum(value_part, axis=0)), lax.optimization_barrier(jnp.sum(state_part, axis=0)))
    attended, query_grad, key_local, value_local, state_grads = lax.map(block_pass, (query_blocks, kv_blocks, grad_blocks, starts))
    suffix = jnp.cumsum(state_grads[::-1], axis=0)[::-1]
    later = jnp.concatenate([suffix[1:], jnp.zeros_like(suffix[:1])], axis=0).astype(jnp.bfloat16)
    init_grad = suffix[0]

    def key_pass(inputs):
        kv_block, later_low = inputs
        keys = kv_block[:, :HEAD_DIM]
        values = kv_block[:, HEAD_DIM:]
        kfeat = features(keys.astype(jnp.float32), tables).astype(jnp.bfloat16)
        value_state = product(kfeat, later_low, ((1,), (1,)))
        d_kfeat = product(values, later_low, ((1,), (0,))).astype(jnp.bfloat16)
        key_state = feature_grad(keys, d_kfeat, tables)
        return (key_state, value_state)
    key_state, value_state = lax.map(key_pass, (kv_blocks, later))
    kv_grad = jnp.concatenate([key_local + key_state, value_local + value_state], axis=2)
    return (attended.reshape(TOKENS, HEADS * HEAD_DIM), query_grad.reshape(TOKENS, HEADS * HEAD_DIM), kv_grad.reshape(TOKENS, 2 * HEAD_DIM).astype(jnp.float32), init_grad)
```

```python
import jax
import jax.numpy as jnp
import numpy as np
from jax import lax
from jax.experimental import pallas as pl
from jax.experimental.pallas import tpu as pltpu
from jax.sharding import PartitionSpec as P

DIM = 64
GROUP = 1024
FEATURES = 2080
EPSILON = 1e-06
WIDTHS = [DIM - 8 * g for g in range(8)]
STARTS = [sum(4 * w for w in WIDTHS[:g]) for g in range(8)]
ROWS = sum(4 * w for w in WIDTHS)
PIECE = ROWS // 8
F32 = jnp.float32
BF16 = jnp.bfloat16
MIB = 1024 * 1024


def weights_of():
    c = np.zeros((ROWS, 128), np.float32)
    for g in range(8):
        for half in range(2):
            for i in range(4):
                a = 8 * g + 4 * half + i
                b = np.arange(8 * g, DIM)
                value = np.where(b == a, 1.0, np.where(b > a, np.sqrt(2.0), 0.0)) / np.sqrt(DIM)
                row = STARTS[g] + i * WIDTHS[g]
                c[row : row + WIDTHS[g], 64 * half : 64 * half + 64] = value[:, None]
    return c


FIRST = weights_of()
SECOND = np.where(FIRST > 0, np.where(FIRST > 0.15, 2.0 / DIM, 1.0 / DIM), 0.0).astype(np.float32)


def triu_start(a):
    return DIM * a - a * (a - 1) // 2


def dot(x, y):
    return lax.dot_general(x, y, (((1,), (0,)), ((), ())), preferred_element_type=F32)


def build_features(x_ref, base, phi_ref, tokens, chunk=128):
    def one(step, carry):
        lanes = pl.ds(pl.multiple_of(step * chunk, chunk), chunk)
        for g in range(8):
            tail = x_ref[pl.ds(base + 8 * g, WIDTHS[g]), lanes]
            for half in range(2):
                parts = []
                for i in range(4):
                    a = 8 * g + 4 * half + i
                    parts.append(tail[a - 8 * g : a - 8 * g + 1, :] * tail)
                block = jnp.concatenate(parts, axis=0).astype(BF16)
                phi_ref[pl.ds(half * ROWS + STARTS[g], 4 * WIDTHS[g]), lanes] = block
        return carry

    lax.fori_loop(0, tokens // chunk, one, 0)


def fold_features(x_ref, base, x_lane, d_ref, rows_ref, out_ref, out_base, tokens):
    def one(step, carry):
        at = pl.multiple_of(step * 128, 128)
        lanes = pl.ds(at, 128)
        xl = pl.ds(pl.multiple_of(x_lane + at, 128), 128)
        x = x_ref[pl.ds(base, DIM), xl]
        acc = [jnp.zeros((8, 128), F32) for _ in range(8)]
        for g in range(8):
            for half in range(2):
                for i in range(4):
                    a = 8 * g + 4 * half + i
                    xa = x[a : a + 1, :]
                    row = half * ROWS + STARTS[g] + i * WIDTHS[g]
                    total = None
                    for k in range(g, 8):
                        d = d_ref[pl.ds(row + 8 * (k - g), 8), lanes]
                        acc[k] = acc[k] + d * xa
                        term = d * x[8 * k : 8 * k + 8, :]
                        total = term if total is None else total + term
                    rows_ref[a : a + 1, :] = jnp.sum(total, axis=0, keepdims=True)
        grad = jnp.concatenate(acc, axis=0) + rows_ref[...]
        out_ref[pl.ds(out_base, DIM), xl] = out_ref[pl.ds(out_base, DIM), xl] + grad
        return carry

    lax.fori_loop(0, tokens // 128, one, 0)


def low_lanes(shape):
    return lax.broadcasted_iota(jnp.int32, shape, 1) < 64


def update_kernel(kv_ref, out_ref, x_ref, phi_ref):
    kv = kv_ref[...]
    x_ref[...] = kv.astype(F32).T
    build_features(x_ref, 0, phi_ref, GROUP)
    v = kv[:, DIM:]
    vv = jnp.concatenate([v, v], axis=1)
    lo = dot(phi_ref[0:ROWS], vv)
    hi = dot(phi_ref[ROWS : 2 * ROWS], vv)
    out_ref[...] = jnp.where(low_lanes((ROWS, 128)), lo, hi)


def init_kernel(init_ref, first_ref, out_ref, t_ref):
    t_ref[...] = jnp.concatenate([init_ref[...], init_ref[...]], axis=0).T
    for g in range(8):
        for i in range(4):
            rows = []
            for half in range(2):
                a = 8 * g + 4 * half + i
                rows.append(t_ref[pl.ds(triu_start(a) - (a - 8 * g), WIDTHS[g]), :])
            at = pl.ds(STARTS[g] + i * WIDTHS[g], WIDTHS[g])
            out_ref[at, :] = jnp.where(low_lanes((WIDTHS[g], 128)), rows[0], rows[1]) * first_ref[at, :]


def causal(rows, j):
    return lax.broadcasted_iota(jnp.int32, (rows, 256), 0) <= lax.broadcasted_iota(jnp.int32, (rows, 256), 1) + 256 * j


def local_kernel(kv_ref, q_ref, out_ref, qt_ref):
    kv = kv_ref[...]
    k = kv[:, :DIM]
    vt = kv.astype(F32).T[DIM:].astype(BF16)
    qt_ref[...] = q_ref[...].astype(F32).T.astype(BF16)

    def head(hh, carry):
        at = pl.ds(pl.multiple_of(hh * DIM, DIM), DIM)
        for j in range(4):
            last = 256 * (j + 1)
            logits = dot(k[:last], qt_ref[at, 256 * j : last])
            w = jnp.where(causal(last, j), logits * logits * (1.0 / DIM), 0.0).astype(BF16)
            out_ref[at, 256 * j : last] = dot(vt[:, :last], w)
        return carry

    lax.fori_loop(0, 4, head, 0)


def place(where_ref, mine_ref, other_ref, out_ref):
    h, c = where_ref[0], where_ref[1]
    for s in range(4):
        base = lax.rem(h - s + 4, 4) * 2
        here = pl.ds(s * PIECE, PIECE)
        out_ref[pl.ds(pl.multiple_of((base + c) * PIECE, 8), PIECE), :] = mine_ref[here, :]
        out_ref[pl.ds(pl.multiple_of((base + 1 - c) * PIECE, 8), PIECE), :] = other_ref[here, :]


def flip_state(state, flat_ref):
    turned = state.T.astype(BF16)
    flat_ref[:, 0:ROWS] = turned[0:DIM]
    flat_ref[:, ROWS : 2 * ROWS] = turned[DIM : 2 * DIM]


def main_kernel(
    where_ref, mine_ref, other_ref, before_ref, init_ref, second_ref, q_ref, g_ref, intra_ref,
    state_out, att_out, dn_out, grad_out,
    sum_ref, flat_ref, qt_ref, gt_ref, phi_ref,
):
    place(where_ref, mine_ref, other_ref, sum_ref)
    core = where_ref[1].astype(F32)
    state = init_ref[...] + second_ref[...] * (sum_ref[...] + core * before_ref[...])
    state_out[...] = state.astype(BF16)
    flip_state(state, flat_ref)
    qt_ref[...] = q_ref[...].astype(F32).T
    gt_ref[...] = g_ref[...].astype(F32).T

    def head(hh, carry):
        base = pl.multiple_of(hh * DIM, DIM)
        at = pl.ds(base, DIM)
        build_features(qt_ref, base, phi_ref, GROUP)
        numer = dot(flat_ref[...], phi_ref[...]) + intra_ref[at, :]
        scale = lax.rsqrt(jnp.mean(numer * numer, axis=0, keepdims=True) + EPSILON)
        y = numer * scale
        u = gt_ref[at, :]
        dn = scale * (u - y * jnp.mean(u * y, axis=0, keepdims=True))
        gt_ref[at, :] = y
        dn_out[at, :] = dn.astype(BF16)
        twice = jnp.concatenate([dn, dn], axis=0).T.astype(BF16)
        lo = dot(phi_ref[0:ROWS], twice)
        hi = dot(phi_ref[ROWS : 2 * ROWS], twice)
        total = jnp.where(low_lanes((ROWS, 128)), lo, hi)

        @pl.when(hh == 0)
        def _():
            grad_out[...] = total

        @pl.when(hh > 0)
        def _():
            grad_out[...] = grad_out[...] + total

        return carry

    lax.fori_loop(0, 4, head, 0)
    att_out[...] = gt_ref[...].T.astype(BF16)


def back_kernel(kv_ref, q_ref, dn_ref, state_ref, qg_out, kvl_out, qt_ref, acc_ref, d_ref, rows_ref):
    kv = kv_ref[...]
    k = kv[:, :DIM]
    v = kv[:, DIM:]
    kt = kv.astype(F32).T[:DIM].astype(BF16)
    q = q_ref[...]
    qt_ref[...] = q.astype(F32).T
    acc_ref[...] = jnp.zeros_like(acc_ref)
    kvl_out[...] = jnp.zeros_like(kvl_out)
    zeros = jnp.zeros((DIM, 256), BF16)
    for hh in range(2):
        for j in range(4):
            first, last = 256 * j, 256 * (j + 1)
            dnt = dn_ref[DIM * hh : DIM * hh + DIM, first:last]
            qt = qt_ref[DIM * hh : DIM * hh + DIM, first:last]
            logits = dot(k[:last], qt.astype(BF16))
            keep = causal(last, j)
            w = jnp.where(keep, logits * logits * (1.0 / DIM), 0.0).astype(BF16)
            dw = dot(v[:last], dnt)
            dl = jnp.where(keep, dw * logits * (2.0 / DIM), 0.0).astype(BF16)
            both = jnp.concatenate([qt, dnt.astype(F32)], axis=0).T.astype(BF16)
            low = low_lanes((256, 128))
            qz = jnp.where(low, both, jnp.zeros_like(both))
            dnz = jnp.where(low, jnp.zeros_like(both), both)
            kvl_out[0:last, :] = kvl_out[0:last, :] + (dot(dl, qz) + dot(w, dnz))
            acc_ref[DIM * hh : DIM * hh + DIM, first:last] = dot(kt[:, :last], dl)
            d_ref[0:ROWS, :] = dot(state_ref[...], jnp.concatenate([dnt, zeros], axis=0))
            d_ref[ROWS : 2 * ROWS, :] = dot(state_ref[...], jnp.concatenate([zeros, dnt], axis=0))
            fold_features(qt_ref, DIM * hh, first, d_ref, rows_ref, acc_ref, DIM * hh, 256)
    qg_out[...] = acc_ref[...].T.astype(BF16)


def key_kernel(
    where_ref, mine_ref, other_ref, amine_ref, aother_ref, second_ref, kv_ref, l0, l1, l2, l3,
    out_ref,
    sum_ref, add_ref, low_ref, flat_ref, x_ref, acc_ref, d_ref, rows_ref, phi_ref,
):
    place(where_ref, mine_ref, other_ref, sum_ref)
    place(where_ref, amine_ref, aother_ref, add_ref)
    lead = 1.0 - where_ref[1].astype(F32)
    state = second_ref[...] * (sum_ref[...] + lead * add_ref[...])
    low_ref[...] = state.astype(BF16)
    flip_state(state, flat_ref)
    x_ref[...] = kv_ref[...].astype(F32).T
    build_features(x_ref, 0, phi_ref, GROUP)
    acc_ref[DIM : 2 * DIM, :] = dot(flat_ref[...], phi_ref[...])
    acc_ref[0:DIM, :] = jnp.zeros((DIM, GROUP), F32)
    zeros = jnp.zeros((DIM, 256), BF16)
    for j in range(4):
        first, last = 256 * j, 256 * (j + 1)
        vt = x_ref[DIM : 2 * DIM, first:last].astype(BF16)
        d_ref[0:ROWS, :] = dot(low_ref[...], jnp.concatenate([vt, zeros], axis=0))
        d_ref[ROWS : 2 * ROWS, :] = dot(low_ref[...], jnp.concatenate([zeros, vt], axis=0))
        fold_features(x_ref, 0, first, d_ref, rows_ref, acc_ref, 0, 256)
    h = where_ref[0]
    for s, part in enumerate((l0, l1, l2, l3)):
        at = pl.ds(pl.multiple_of(lax.rem(h - s + 4, 4) * 256, 256), 256)
        out_ref[at, :] = part[...]
    out_ref[...] = out_ref[...] + acc_ref[...].T


def total_kernel(where_ref, mine_ref, other_ref, first_ref, out_ref, sum_ref, t_ref):
    place(where_ref, mine_ref, other_ref, sum_ref)
    for a in reversed(range(DIM)):
        g = a // 8
        i, half = a % 4, (a % 8) // 4
        at = pl.ds(STARTS[g] + i * WIDTHS[g], WIDTHS[g])
        piece = sum_ref[at, :] * first_ref[at, :]
        if half:
            piece = pltpu.roll(piece, 64, 1)
        t_ref[pl.ds(triu_start(a) - (a - 8 * g), WIDTHS[g]), :] = piece
    width = FEATURES // 4
    mine = t_ref[pl.ds(pl.multiple_of(where_ref[0] * width, 8), width), :]
    out_ref[...] = mine.T[0:DIM]


def vmem(shape, kind=F32):
    return pltpu.VMEM(shape, kind)


def call(kernel, outs, scratch, args, scalar=False, limit=40):
    specs = [pl.BlockSpec(memory_space=pltpu.VMEM) for _ in args]
    if scalar:
        specs[0] = pl.BlockSpec(memory_space=pltpu.SMEM)
    return pl.pallas_call(
        kernel,
        out_shape=[jax.ShapeDtypeStruct(s, k) for s, k in outs],
        in_specs=specs,
        out_specs=[pl.BlockSpec(memory_space=pltpu.VMEM) for _ in outs],
        scratch_shapes=scratch,
        compiler_params=pltpu.CompilerParams(vmem_limit_bytes=limit * MIB),
    )(*args)


def shift_pairs(axis, s):
    pairs = []
    for j in range(32):
        y, z, c = j // 8, (j // 2) % 4, j % 2
        if axis == "y":
            y = (y + s) % 4
        elif axis == "z":
            z = (z + s) % 4
        else:
            c = 1 - c
        pairs.append((j, y * 8 + z * 2 + c))
    return pairs


def move(x, axis, s=1):
    if axis == "x":
        return lax.ppermute(x, "head", [(j, (j + s) % 4) for j in range(4)])
    return lax.ppermute(x, "seq", shift_pairs(axis, s))


def take(x, index, rows):
    return lax.dynamic_slice_in_dim(x, index * rows, rows, 0)


def gather_state(piece):
    stack = jnp.concatenate([piece] + [move(piece, "x", s) for s in (1, 2, 3)], axis=0)
    return stack, move(stack, "c")


def scan_chips(total, place_z, place_y, sign):
    recv = [move(total, "z", sign * s) for s in (1, 2, 3)]
    part = jnp.zeros_like(total)
    plane = total
    for s, r in zip((1, 2, 3), recv):
        part = part + jnp.where(place_z >= s, r, 0.0)
        plane = plane + r
    recv = [move(plane, "y", sign * s) for s in (1, 2, 3)]
    every = plane
    for s, r in zip((1, 2, 3), recv):
        part = part + jnp.where(place_y >= s, r, 0.0)
        every = every + r
    return part, every


def per_device(queries, keys_values, init_state, out_grad):
    h = lax.axis_index("head")
    seq = lax.axis_index("seq")
    c, z, y = seq % 2, (seq // 2) % 4, seq // 8
    where = jnp.stack([h, c]).astype(jnp.int32)
    first, second = jnp.asarray(FIRST), jnp.asarray(SECOND)

    (update,) = call(
        update_kernel, [((ROWS, 128), F32)], [vmem((128, GROUP)), vmem((2 * ROWS, GROUP), BF16)], [keys_values]
    )
    other_update = move(update, "c")
    chip = take(update, h * 2 + c, PIECE) + take(other_update, h * 2 + c, PIECE)
    before, _ = scan_chips(chip, z, y, 1)
    mine, other = gather_state(before)

    (init_low,) = call(init_kernel, [((ROWS, 128), F32)], [vmem((FEATURES, 128))], [init_state, first])
    (intra,) = call(
        local_kernel, [((4 * DIM, GROUP), F32)], [vmem((4 * DIM, GROUP), BF16)], [keys_values, queries]
    )
    state, attended, dn, grads = call(
        main_kernel,
        [((ROWS, 128), BF16), ((GROUP, 4 * DIM), BF16), ((4 * DIM, GROUP), BF16), ((ROWS, 128), F32)],
        [
            vmem((ROWS, 128)),
            vmem((DIM, 2 * ROWS), BF16),
            vmem((4 * DIM, GROUP)),
            vmem((4 * DIM, GROUP)),
            vmem((2 * ROWS, GROUP), BF16),
        ],
        [where, mine, other, other_update, init_low, second, queries, out_grad, intra],
        scalar=True,
    )

    own = take(grads, h, 2 * PIECE)
    for s in (1, 2, 3):
        own = own + move(take(grads, (h + s) % 4, 2 * PIECE), "x", s)
    other_own = move(own, "c")
    chip_grad = take(own, c, PIECE) + take(other_own, c, PIECE)
    later_core = jnp.where(c == 1, take(own, c, PIECE), take(other_own, c, PIECE))
    after, every = scan_chips(chip_grad, 3 - z, 3 - y, -1)
    mine_after, other_after = gather_state(after)
    mine_core, other_core = gather_state(later_core)
    mine_every, other_every = gather_state(every)

    def back(p):
        return call(
            back_kernel,
            [((GROUP, 128), BF16), ((GROUP, 128), F32)],
            [vmem((128, GROUP)), vmem((128, GROUP)), vmem((2 * ROWS, 256)), vmem((DIM, 128))],
            [keys_values, queries[:, 128 * p : 128 * p + 128], dn[128 * p : 128 * p + 128], state],
        )

    grad0, local0 = back(0)
    grad1, local1 = back(1)
    query_grad = jnp.concatenate([grad0, grad1], axis=1)
    local = local0 + local1
    part = take(local, h, 256)
    for s in (1, 2, 3):
        part = part + move(take(local, (h + s) % 4, 256), "x", s)
    parts = [part] + [move(part, "x", s) for s in (1, 2, 3)]

    (kv_grad,) = call(
        key_kernel,
        [((GROUP, 128), F32)],
        [
            vmem((ROWS, 128)),
            vmem((ROWS, 128)),
            vmem((ROWS, 128), BF16),
            vmem((DIM, 2 * ROWS), BF16),
            vmem((128, GROUP)),
            vmem((128, GROUP)),
            vmem((2 * ROWS, 256)),
            vmem((DIM, 128)),
            vmem((2 * ROWS, GROUP), BF16),
        ],
        [where, mine_after, other_after, mine_core, other_core, second, keys_values] + parts,
        scalar=True,
    )
    (init_grad,) = call(
        total_kernel,
        [((DIM, FEATURES // 4), F32)],
        [vmem((ROWS, 128)), vmem((FEATURES, 128))],
        [where, mine_every, other_every, first],
        scalar=True,
    )
    return attended, query_grad, kv_grad, init_grad


def solution(mesh):
    return jax.shard_map(
        per_device,
        mesh=mesh,
        in_specs=(P("seq", "head"), P("seq", None), P(), P("seq", "head")),
        out_specs=(P("seq", "head"), P("seq", "head"), P("seq", None), P(None, "head")),
        check_vma=False,
    )
```

```python
import functools

import jax
import jax.numpy as jnp
import numpy as np
from jax import lax
from jax.experimental import pallas as pl
from jax.experimental.pallas import tpu as pltpu
from jax.sharding import PartitionSpec as P

DIM = 64
GROUP = 1024
FEATURES = 2080
EPSILON = 1e-06
WIDTHS = [DIM - 8 * g for g in range(8)]
STARTS = [sum(4 * w for w in WIDTHS[:g]) for g in range(8)]
ROWS = sum(4 * w for w in WIDTHS)
PIECE = ROWS // 8
F32 = jnp.float32
BF16 = jnp.bfloat16
MIB = 1024 * 1024


def weights_of():
    c = np.zeros((ROWS, 128), np.float32)
    for g in range(8):
        for half in range(2):
            for i in range(4):
                a = 8 * g + 4 * half + i
                b = np.arange(8 * g, DIM)
                value = np.where(b == a, 1.0, np.where(b > a, np.sqrt(2.0), 0.0)) / np.sqrt(DIM)
                row = STARTS[g] + i * WIDTHS[g]
                c[row : row + WIDTHS[g], 64 * half : 64 * half + 64] = value[:, None]
    return c


FIRST = weights_of()
SECOND = np.where(FIRST > 0, np.where(FIRST > 0.15, 2.0 / DIM, 1.0 / DIM), 0.0).astype(np.float32)


def triu_start(a):
    return DIM * a - a * (a - 1) // 2


def dot(x, y):
    return lax.dot_general(x, y, (((1,), (0,)), ((), ())), preferred_element_type=F32)


def build_features(x_ref, base, phi_ref, tokens, start=0):
    def one(step, carry):
        lanes = pl.ds(pl.multiple_of(start + step * 128, 128), 128)
        for g in range(8):
            tail = x_ref[pl.ds(base + 8 * g, WIDTHS[g]), lanes]
            for half in range(2):
                parts = []
                for i in range(4):
                    a = 8 * g + 4 * half + i
                    parts.append(tail[a - 8 * g : a - 8 * g + 1, :] * tail)
                block = jnp.concatenate(parts, axis=0).astype(BF16)
                phi_ref[pl.ds(half * ROWS + STARTS[g], 4 * WIDTHS[g]), lanes] = block
        return carry

    lax.fori_loop(0, tokens // 128, one, 0)


def fold_step(x_ref, base, x_lane, d_ref, rows_ref, out_ref, out_base, at):
    lanes = pl.ds(at, 128)
    xl = pl.ds(x_lane + at, 128)
    x = x_ref[pl.ds(base, DIM), xl]
    acc = [jnp.zeros((8, 128), F32) for _ in range(8)]
    for g in range(8):
        for half in range(2):
            for i in range(4):
                a = 8 * g + 4 * half + i
                xa = x[a : a + 1, :]
                row = half * ROWS + STARTS[g] + i * WIDTHS[g]
                total = None
                for k in range(g, 8):
                    d = d_ref[pl.ds(row + 8 * (k - g), 8), lanes]
                    acc[k] = acc[k] + d * xa
                    term = d * x[8 * k : 8 * k + 8, :]
                    total = term if total is None else total + term
                rows_ref[a : a + 1, :] = jnp.sum(total, axis=0, keepdims=True)
    grad = jnp.concatenate(acc, axis=0) + rows_ref[...]
    out_ref[pl.ds(out_base, DIM), xl] = out_ref[pl.ds(out_base, DIM), xl] + grad


def low_lanes(shape):
    return lax.broadcasted_iota(jnp.int32, shape, 1) < 64


def update_kernel(kv_hbm, out_ref, x_ref, phi_ref, kv_ref, sems):
    fetch([(kv_hbm, kv_ref)], sems)[0].wait()
    kv = kv_ref[...]
    x_ref[...] = kv.astype(F32).T
    build_features(x_ref, 0, phi_ref, GROUP)
    v = kv[:, DIM:]
    vv = jnp.concatenate([v, v], axis=1)
    lo = dot(phi_ref[0:ROWS], vv)
    hi = dot(phi_ref[ROWS : 2 * ROWS], vv)
    out_ref[...] = jnp.where(low_lanes((ROWS, 128)), lo, hi)


def fetch(pairs, sems):
    copies = [pltpu.make_async_copy(a, b, sems.at[i]) for i, (a, b) in enumerate(pairs)]
    for copy in copies:
        copy.start()
    return copies


def init_kernel(init_hbm, first_hbm, out_ref, t_ref, init_ref, first_ref, sems):
    for copy in fetch([(init_hbm, init_ref), (first_hbm, first_ref)], sems):
        copy.wait()
    t_ref[...] = jnp.concatenate([init_ref[...], init_ref[...]], axis=0).T
    for g in range(8):
        for i in range(4):
            rows = []
            for half in range(2):
                a = 8 * g + 4 * half + i
                rows.append(t_ref[pl.ds(triu_start(a) - (a - 8 * g), WIDTHS[g]), :])
            at = pl.ds(STARTS[g] + i * WIDTHS[g], WIDTHS[g])
            out_ref[at, :] = jnp.where(low_lanes((WIDTHS[g], 128)), rows[0], rows[1]) * first_ref[at, :]


def causal(rows, j):
    return lax.broadcasted_iota(jnp.int32, (rows, 256), 0) <= lax.broadcasted_iota(jnp.int32, (rows, 256), 1) + 256 * j


def local_kernel(kv_ref, q_ref, out_ref, qt_ref):
    kv = kv_ref[...]
    k = kv[:, :DIM]
    vt = kv.astype(F32).T[DIM:].astype(BF16)
    qt_ref[...] = q_ref[...].astype(F32).T.astype(BF16)
    for hh in range(2):
        at = slice(hh * DIM, hh * DIM + DIM)
        for j in range(4):
            last = 256 * (j + 1)
            logits = dot(k[:last], qt_ref[at, 256 * j : last])
            w = jnp.where(causal(last, j), logits * logits * (1.0 / DIM), 0.0).astype(BF16)
            out_ref[at, 256 * j : last] = dot(vt[:, :last], w)


def feature_kernel(hh, q_ref, out_ref, x_ref, phi_ref, sems):
    x_ref[...] = q_ref[...].astype(F32).T
    copies = []
    for j in range(4):
        build_features(x_ref, DIM * hh, phi_ref, 256, 256 * j)
        lanes = pl.ds(256 * j, 256)
        copies.append(pltpu.make_async_copy(phi_ref.at[:, lanes], out_ref.at[:, lanes], sems.at[j]))
        copies[j].start()
    for copy in copies:
        copy.wait()


def sources(h):
    near = h + 1 - 2 * lax.rem(h, 2)
    return h, near, 3 - h, 3 - near


def place(where_ref, mine_ref, other_ref, out_ref):
    h, c = where_ref[0], where_ref[1]
    for s, source in enumerate(sources(h)):
        here = pl.ds(s * PIECE, PIECE)
        out_ref[pl.ds(pl.multiple_of((source * 2 + c) * PIECE, 8), PIECE), :] = mine_ref[here, :]
        out_ref[pl.ds(pl.multiple_of((source * 2 + 1 - c) * PIECE, 8), PIECE), :] = other_ref[here, :]


def flip_state(state, flat_ref):
    turned = state.T.astype(BF16)
    flat_ref[:, 0:ROWS] = turned[0:DIM]
    flat_ref[:, ROWS : 2 * ROWS] = turned[DIM : 2 * DIM]


def main_kernel(
    where_ref, mine_ref, other_ref, before_ref, init_ref, second_hbm, grad_hbm, intra0_ref, intra1_ref, f0, f1, f2, f3,
    state_out, att_out, dn_out, g0, g1, g2, g3,
    sum_ref, flat_ref, gt_ref, grad_ref, phi_ref, sems, second_ref, q_ref, more_sems,
):
    small = fetch([(second_hbm, second_ref), (grad_hbm, q_ref)], more_sems)
    copies = [pltpu.make_async_copy(f, phi_ref.at[i % 2], sems.at[i]) for i, f in enumerate((f0, f1, f2, f3))]
    copies[0].start()
    copies[1].start()
    place(where_ref, mine_ref, other_ref, sum_ref)
    core = where_ref[1].astype(F32)
    for copy in small:
        copy.wait()
    state = init_ref[...] + second_ref[...] * (sum_ref[...] + core * before_ref[...])
    state_out[...] = state.astype(BF16)
    flip_state(state, flat_ref)
    gt_ref[...] = q_ref[...].astype(F32).T
    for hh in range(4):
        at = slice(hh * DIM, hh * DIM + DIM)
        copies[hh].wait()
        slot = hh % 2
        intra_ref = (intra0_ref, intra1_ref)[hh // 2]
        half = slice((hh % 2) * DIM, (hh % 2) * DIM + DIM)
        numer = dot(flat_ref[...], phi_ref[slot]) + intra_ref[half, :]
        scale = lax.rsqrt(jnp.mean(numer * numer, axis=0, keepdims=True) + EPSILON)
        y = numer * scale
        u = gt_ref[at, :]
        dn = scale * (u - y * jnp.mean(u * y, axis=0, keepdims=True))
        gt_ref[at, :] = y
        dn_out[at, :] = dn.astype(BF16)
        twice = jnp.concatenate([dn, dn], axis=0).T.astype(BF16)
        lo = dot(phi_ref[slot, 0:ROWS], twice)
        hi = dot(phi_ref[slot, ROWS : 2 * ROWS], twice)
        total = jnp.where(low_lanes((ROWS, 128)), lo, hi)
        grad_ref[...] = total if hh == 0 else grad_ref[...] + total
        if hh < 2:
            copies[hh + 2].start()
    for s, out in enumerate((g0, g1, g2, g3)):
        at = pl.multiple_of(lax.rem(where_ref[0] + s, 4) * 2 * PIECE, 8)
        out[...] = grad_ref[pl.ds(at, 2 * PIECE), :]
    att_out[...] = gt_ref[...].T.astype(BF16)


def back_local_kernel(kv_ref, q_ref, dn_ref, qg_out, kvl_out, qt_ref):
    kv = kv_ref[...]
    k = kv[:, :DIM]
    v = kv[:, DIM:]
    kt = kv.astype(F32).T[:DIM].astype(BF16)
    qt_ref[...] = q_ref[...].astype(F32).T
    kvl_out[...] = jnp.zeros_like(kvl_out)
    low = low_lanes((256, 128))

    def head(hh, carry):
        at = pl.ds(pl.multiple_of(hh * DIM, DIM), DIM)
        for j in range(4):
            first, last = 256 * j, 256 * (j + 1)
            dnt = dn_ref[at, first:last]
            qt = qt_ref[at, first:last]
            logits = dot(k[:last], qt.astype(BF16))
            keep = causal(last, j)
            w = jnp.where(keep, logits * logits * (1.0 / DIM), 0.0).astype(BF16)
            dw = dot(v[:last], dnt)
            dl = jnp.where(keep, dw * logits * (2.0 / DIM), 0.0).astype(BF16)
            both = jnp.concatenate([qt, dnt.astype(F32)], axis=0).T.astype(BF16)
            qz = jnp.where(low, both, jnp.zeros_like(both))
            dnz = jnp.where(low, jnp.zeros_like(both), both)
            kvl_out[0:last, :] = kvl_out[0:last, :] + (dot(dl, qz) + dot(w, dnz))
            qg_out[at, first:last] = dot(kt[:, :last], dl)
        return carry

    lax.fori_loop(0, 4, head, 0)


def back_state_kernel(q_ref, dn_ref, state_ref, local_ref, *rest):
    out_ref, qt_ref, acc_ref, da_ref, db_ref, ra_ref, rb_ref = rest[-7:]
    qt_ref[...] = q_ref[...].astype(F32).T
    acc_ref[...] = local_ref[...]
    zeros = jnp.zeros((DIM, 256), BF16)

    def spread(hh, d_ref):
        dnt = dn_ref[hh * DIM : hh * DIM + DIM, :]
        d_ref[0:ROWS, :] = dot(state_ref[...], jnp.concatenate([dnt, zeros], axis=0))
        d_ref[ROWS : 2 * ROWS, :] = dot(state_ref[...], jnp.concatenate([zeros, dnt], axis=0))

    spread(0, da_ref)
    for hh in range(4):
        now, then = ((da_ref, db_ref), (db_ref, da_ref))[hh % 2]
        if hh < 3:
            spread(hh + 1, then)
        for step in range(2):
            fold_step(qt_ref, DIM * hh, 0, now, (ra_ref, rb_ref)[step], acc_ref, DIM * hh, 128 * step)
    out_ref[...] = acc_ref[...].T.astype(BF16)


def place_wide(where_ref, near_ref, far_ref, out_ref):
    for s, source in enumerate(sources(where_ref[0])):
        held = (near_ref, near_ref, far_ref, far_ref)[s]
        at = (s % 2) * 2 * PIECE
        out_ref[pl.ds(pl.multiple_of(source * 2 * PIECE, 8), 2 * PIECE), :] = held[at : at + 2 * PIECE, :]


def key_kernel(
    where_ref, near_ref, far_ref, second_ref, kv_ref, kv_mine_ref, kv_other_ref,
    out_ref,
    sum_ref, low_ref, flat_ref, x_ref, acc_ref, da_ref, db_ref, ra_ref, rb_ref, phi_ref,
):
    place_wide(where_ref, near_ref, far_ref, sum_ref)
    state = second_ref[...] * sum_ref[...]
    low_ref[...] = state.astype(BF16)
    flip_state(state, flat_ref)
    x_ref[...] = kv_ref[...].astype(F32).T
    build_features(x_ref, 0, phi_ref, GROUP)
    acc_ref[0:DIM, :] = jnp.zeros((DIM, GROUP), F32)
    zeros = jnp.zeros((DIM, 256), BF16)

    def spread(j, d_ref):
        vt = x_ref[DIM : 2 * DIM, 256 * j : 256 * j + 256].astype(BF16)
        d_ref[0:ROWS, :] = dot(low_ref[...], jnp.concatenate([vt, zeros], axis=0))
        d_ref[ROWS : 2 * ROWS, :] = dot(low_ref[...], jnp.concatenate([zeros, vt], axis=0))

    spread(0, da_ref)
    for j in range(4):
        now, then = ((da_ref, db_ref), (db_ref, da_ref))[j % 2]
        if j < 3:
            spread(j + 1, then)
        else:
            acc_ref[DIM : 2 * DIM, :] = dot(flat_ref[...], phi_ref[...])
        for step in range(2):
            fold_step(x_ref, 0, 256 * j, now, (ra_ref, rb_ref)[step], acc_ref, 0, 128 * step)
    out_ref[...] = (kv_mine_ref[...] + kv_other_ref[...]) + acc_ref[...].T


def total_kernel(where_ref, near_ref, far_ref, first_ref, out_ref, sum_ref, t_ref):
    place_wide(where_ref, near_ref, far_ref, sum_ref)
    for a in reversed(range(DIM)):
        g = a // 8
        i, half = a % 4, (a % 8) // 4
        at = pl.ds(STARTS[g] + i * WIDTHS[g], WIDTHS[g])
        piece = sum_ref[at, :] * first_ref[at, :]
        if half:
            piece = pltpu.roll(piece, 64, 1)
        t_ref[pl.ds(triu_start(a) - (a - 8 * g), WIDTHS[g]), :] = piece
    width = FEATURES // 4
    mine = t_ref[pl.ds(pl.multiple_of(where_ref[0] * width, 8), width), :]
    out_ref[...] = mine.T[0:DIM]


def vmem(shape, kind=F32):
    return pltpu.VMEM(shape, kind)


WHOLE = pl.BlockSpec(memory_space=pltpu.VMEM)
SCALAR = pl.BlockSpec(memory_space=pltpu.SMEM)
LEFT = pl.BlockSpec(memory_space=pltpu.HBM)


def block(shape, at):
    return pl.BlockSpec(shape, lambda i: at)


def call(kernel, outs, scratch, args, specs=None, out_specs=None, grid=(), aliases=None, limit=40):
    specs = specs or [WHOLE] * len(args)
    out_specs = out_specs or [WHOLE] * len(outs)
    args = [pltpu.with_memory_space_constraint(a, pltpu.HBM) if s is LEFT else a for a, s in zip(args, specs)]
    return pl.pallas_call(
        kernel,
        grid=grid,
        out_shape=[pltpu.HBM(s, k) if o is LEFT else jax.ShapeDtypeStruct(s, k) for (s, k), o in zip(outs, out_specs)],
        in_specs=specs,
        out_specs=out_specs,
        scratch_shapes=scratch,
        input_output_aliases=aliases or {},
        compiler_params=pltpu.CompilerParams(vmem_limit_bytes=limit * MIB),
    )(*args)


PAIRS = {
    "c": lambda x, y, z, c: (x, y, z, 1 - c),
    "z0": lambda x, y, z, c: (x, y, z ^ 1, c),
    "z1": lambda x, y, z, c: (x, y, 3 - z, c),
    "y0": lambda x, y, z, c: (x, y ^ 1, z, c),
    "y1": lambda x, y, z, c: (x, 3 - y, z, c),
}


def move(x, step):
    if step in PAIRS:
        pairs = []
        for j in range(32):
            _, y, z, c = PAIRS[step](0, j // 8, (j // 2) % 4, j % 2)
            pairs.append((j, y * 8 + z * 2 + c))
        return lax.ppermute(x, "seq", pairs)
    if step == "x0":
        return lax.ppermute(x, "head", [(j, j ^ 1) for j in range(4)])
    if step == "x1":
        return lax.ppermute(x, "head", [(j, 3 - j) for j in range(4)])
    return lax.ppermute(x, "head", [(j, (j + step) % 4) for j in range(4)])


def take(x, index, rows):
    return lax.dynamic_slice_in_dim(x, index * rows, rows, 0)


def tie(x, *others):
    return lax.optimization_barrier((x,) + others)[0]


def per_device(queries, keys_values, init_state, out_grad):
    h = lax.axis_index("head")
    seq = lax.axis_index("seq")
    c, z, y = seq % 2, (seq // 2) % 4, seq // 8
    where = jnp.stack([h, c]).astype(jnp.int32)
    first, second = jnp.asarray(FIRST), jnp.asarray(SECOND)
    half = h * 2 + c

    def features_of(hh, q):
        return call(
            functools.partial(feature_kernel, hh % 2),
            [((2 * ROWS, GROUP), BF16)],
            [vmem((128, GROUP)), vmem((2 * ROWS, GROUP), BF16), pltpu.SemaphoreType.DMA((4,))],
            [q],
            specs=[block((GROUP, 128), (0, hh // 2))],
            out_specs=[LEFT],
            grid=(1,),
            limit=10,
        )[0]

    def local_of(p, q):
        return call(
            local_kernel,
            [((128, GROUP), F32)],
            [vmem((128, GROUP), BF16)],
            [keys_values, q],
            specs=[WHOLE, block((GROUP, 128), (0, p))],
            out_specs=[block((128, GROUP), (0, 0))],
            grid=(1,),
            limit=10,
        )[0]

    (update,) = call(
        update_kernel,
        [((ROWS, 128), F32)],
        [
            vmem((128, GROUP)), vmem((2 * ROWS, GROUP), BF16), vmem((GROUP, 128), BF16), pltpu.SemaphoreType.DMA((1,)),
        ],
        [keys_values],
        specs=[LEFT],
        limit=12,
    )
    (init_low,) = call(
        init_kernel,
        [((ROWS, 128), F32)],
        [
            vmem((FEATURES, 128)), vmem((DIM, FEATURES)), vmem((ROWS, 128)), pltpu.SemaphoreType.DMA((2,)),
        ],
        [tie(init_state, update), first],
        specs=[LEFT, LEFT],
        limit=8,
    )
    other_update = move(update, "c")
    chip = take(update, half, PIECE) + take(other_update, half, PIECE)
    chip = tie(chip, init_low)
    feats = [None] * 4
    feats[0] = features_of(0, tie(queries, chip))
    got = move(chip, "z0")
    part = jnp.where(z % 2 == 1, got, 0.0)
    total = tie(chip + got, feats[0])
    feats[1] = features_of(1, tie(queries, total))
    got = move(total, "z1")
    part = part + jnp.where(z >= 2, got, 0.0)
    total = tie(total + got, feats[1])
    feats[2] = features_of(2, tie(queries, total))
    got = move(total, "y0")
    part = part + jnp.where(y % 2 == 1, got, 0.0)
    total = tie(total + got, feats[2])
    intra0 = local_of(0, tie(queries, total))
    got = move(total, "y1")
    part = tie(part + jnp.where(y >= 2, got, 0.0), intra0)
    intra1 = local_of(1, tie(queries, part))
    stack = jnp.concatenate([part, move(part, "x0")], axis=0)
    stack = tie(stack, intra1)
    feats[3] = features_of(3, tie(queries, stack))
    stack = jnp.concatenate([stack, move(stack, "x1")], axis=0)
    stack = tie(stack, feats[3])
    other = move(stack, "c")

    state, attended, dn, mine, *sends = call(
        main_kernel,
        [((ROWS, 128), BF16), ((GROUP, 4 * DIM), BF16), ((4 * DIM, GROUP), BF16)] + [((2 * PIECE, 128), F32)] * 4,
        [
            vmem((ROWS, 128)),
            vmem((DIM, 2 * ROWS), BF16),
            vmem((4 * DIM, GROUP)),
            vmem((ROWS, 128)),
            vmem((2, 2 * ROWS, GROUP), BF16),
            pltpu.SemaphoreType.DMA((4,)),
            vmem((ROWS, 128)),
            vmem((GROUP, 4 * DIM), BF16),
            pltpu.SemaphoreType.DMA((2,)),
        ],
        [where, stack, other, other_update, init_low, second, out_grad, intra0, intra1] + feats,
        specs=[SCALAR] + [WHOLE] * 4 + [LEFT] * 2 + [WHOLE] * 2 + [LEFT] * 4,
        limit=20,
    )

    qg_local, kv_local = call(
        back_local_kernel,
        [((4 * DIM, GROUP), F32), ((GROUP, 128), F32)],
        [vmem((4 * DIM, GROUP))],
        [keys_values, queries, dn],
        limit=16,
    )
    own = mine + move(sends[0], 1) + move(sends[1], 2) + move(sends[2], 3)
    own = tie(own, kv_local)
    other_own = move(own, "c")
    chip = own + other_own
    core_grad = jnp.where(c == 0, other_own, 0.0)

    def state_part(j, dn, before):
        extra = [] if before is None else [before]
        return call(
            back_state_kernel,
            [((GROUP, 4 * DIM), BF16)],
            [vmem((4 * DIM, 256))] * 2 + [vmem((2 * ROWS, 256))] * 2 + [vmem((DIM, 128))] * 2,
            [queries, dn, state, qg_local] + extra,
            specs=[block((256, 256), (j, 0)), block((256, 256), (0, j)), WHOLE, block((256, 256), (0, j))]
            + [LEFT] * len(extra),
            out_specs=[block((256, 256), (j, 0))],
            grid=(1,),
            aliases={4: 0} if extra else None,
            limit=12,
        )[0]

    got = move(chip, "z0")
    kv_got = move(tie(kv_local, chip), "x0")
    qg = state_part(0, tie(dn, chip), None)
    part = core_grad + jnp.where(z % 2 == 0, got, 0.0)
    total = tie(chip + got, qg)

    got = move(total, "z1")
    qg = state_part(1, tie(dn, total), qg)
    part = part + jnp.where(z < 2, got, 0.0)
    kv_pair = tie(kv_local, qg) + kv_got
    total = tie(total + got, qg, kv_pair)

    got = move(total, "y0")
    kv_other = move(tie(kv_pair, total), "x1")
    qg = state_part(2, tie(dn, total), qg)
    part = part + jnp.where(y % 2 == 0, got, 0.0)
    total = tie(total + got, qg)

    got = move(total, "y1")
    qg = state_part(3, tie(dn, total), qg)
    part = tie(part + jnp.where(y < 2, got, 0.0), qg, kv_other)
    every = total + got

    near = jnp.concatenate([part, move(part, "x0")], axis=0)
    every = tie(every, near)
    far = move(near, "x1")
    every_near = jnp.concatenate([every, move(every, "x0")], axis=0)
    every_near = tie(every_near, far)
    every_far = move(every_near, "x1")

    (kv_grad,) = call(
        key_kernel,
        [((GROUP, 128), F32)],
        [vmem((ROWS, 128)), vmem((ROWS, 128), BF16), vmem((DIM, 2 * ROWS), BF16), vmem((128, GROUP)), vmem((128, GROUP))]
        + [vmem((2 * ROWS, 256))] * 2
        + [vmem((DIM, 128))] * 2
        + [vmem((2 * ROWS, GROUP), BF16)],
        [where, near, far, second, keys_values, kv_pair, kv_other],
        specs=[SCALAR] + [WHOLE] * 6,
        limit=20,
    )
    (init_grad,) = call(
        total_kernel,
        [((DIM, FEATURES // 4), F32)],
        [vmem((ROWS, 128)), vmem((FEATURES, 128))],
        [where, every_near, tie(every_far, kv_grad), first],
        specs=[SCALAR] + [WHOLE] * 3,
        limit=8,
    )
    return attended, qg, kv_grad, init_grad


def solution(mesh):
    return jax.shard_map(
        per_device,
        mesh=mesh,
        in_specs=(P("seq", "head"), P("seq", None), P(), P("seq", "head")),
        out_specs=(P("seq", "head"), P("seq", "head"), P("seq", None), P(None, "head")),
        check_vma=False,
    )
```

```python
import functools

import jax
import jax.numpy as jnp
import numpy as np
from jax import lax
from jax.experimental import pallas as pl
from jax.experimental.pallas import tpu as pltpu
from jax.sharding import PartitionSpec as P

DIM = 64
GROUP = 1024
FEATURES = 2080
EPSILON = 1e-06
WIDTHS = [DIM - 8 * g for g in range(8)]
STARTS = [sum(4 * w for w in WIDTHS[:g]) for g in range(8)]
ROWS = sum(4 * w for w in WIDTHS)
PIECE = ROWS // 8
F32 = jnp.float32
BF16 = jnp.bfloat16
MIB = 1024 * 1024


def weights_of():
    c = np.zeros((ROWS, 128), np.float32)
    for g in range(8):
        for half in range(2):
            for i in range(4):
                a = 8 * g + 4 * half + i
                b = np.arange(8 * g, DIM)
                value = np.where(b == a, 1.0, np.where(b > a, np.sqrt(2.0), 0.0)) / np.sqrt(DIM)
                row = STARTS[g] + i * WIDTHS[g]
                c[row : row + WIDTHS[g], 64 * half : 64 * half + 64] = value[:, None]
    return c


FIRST = weights_of()
SECOND = np.where(FIRST > 0, np.where(FIRST > 0.15, 2.0 / DIM, 1.0 / DIM), 0.0).astype(np.float32)


def triu_start(a):
    return DIM * a - a * (a - 1) // 2


def dot(x, y):
    return lax.dot_general(x, y, (((1,), (0,)), ((), ())), preferred_element_type=F32)


def build_features(x_ref, base, phi_ref, tokens, start=0):
    def one(step, carry):
        lanes = pl.ds(pl.multiple_of(start + step * 128, 128), 128)
        for g in range(8):
            tail = x_ref[pl.ds(base + 8 * g, WIDTHS[g]), lanes]
            for half in range(2):
                parts = []
                for i in range(4):
                    a = 8 * g + 4 * half + i
                    parts.append(tail[a - 8 * g : a - 8 * g + 1, :] * tail)
                block = jnp.concatenate(parts, axis=0).astype(BF16)
                phi_ref[pl.ds(half * ROWS + STARTS[g], 4 * WIDTHS[g]), lanes] = block
        return carry

    lax.fori_loop(0, tokens // 128, one, 0)


def fold_step(x_ref, base, x_lane, d_ref, rows_ref, out_ref, out_base, at):
    lanes = pl.ds(at, 128)
    xl = pl.ds(x_lane + at, 128)
    x = x_ref[pl.ds(base, DIM), xl]
    acc = [jnp.zeros((8, 128), F32) for _ in range(8)]
    for g in range(8):
        for half in range(2):
            for i in range(4):
                a = 8 * g + 4 * half + i
                xa = x[a : a + 1, :]
                row = half * ROWS + STARTS[g] + i * WIDTHS[g]
                total = None
                for k in range(g, 8):
                    d = d_ref[pl.ds(row + 8 * (k - g), 8), lanes]
                    acc[k] = acc[k] + d * xa
                    term = d * x[8 * k : 8 * k + 8, :]
                    total = term if total is None else total + term
                rows_ref[a : a + 1, :] = jnp.sum(total, axis=0, keepdims=True)
    grad = jnp.concatenate(acc, axis=0) + rows_ref[...]
    out_ref[pl.ds(out_base, DIM), xl] = out_ref[pl.ds(out_base, DIM), xl] + grad


def low_lanes(shape):
    return lax.broadcasted_iota(jnp.int32, shape, 1) < 64


def update_kernel(kv_hbm, out_ref, x_ref, phi_ref, kv_ref, sems):
    fetch([(kv_hbm, kv_ref)], sems)[0].wait()
    kv = kv_ref[...]
    x_ref[...] = kv.astype(F32).T
    build_features(x_ref, 0, phi_ref, GROUP)
    v = kv[:, DIM:]
    vv = jnp.concatenate([v, v], axis=1)
    lo = dot(phi_ref[0:ROWS], vv)
    hi = dot(phi_ref[ROWS : 2 * ROWS], vv)
    out_ref[...] = jnp.where(low_lanes((ROWS, 128)), lo, hi)


def fetch(pairs, sems):
    copies = [pltpu.make_async_copy(a, b, sems.at[i]) for i, (a, b) in enumerate(pairs)]
    for copy in copies:
        copy.start()
    return copies


def init_kernel(init_hbm, first_hbm, out_ref, t_ref, init_ref, first_ref, sems):
    for copy in fetch([(init_hbm, init_ref), (first_hbm, first_ref)], sems):
        copy.wait()
    t_ref[...] = jnp.concatenate([init_ref[...], init_ref[...]], axis=0).T
    for g in range(8):
        for i in range(4):
            rows = []
            for half in range(2):
                a = 8 * g + 4 * half + i
                rows.append(t_ref[pl.ds(triu_start(a) - (a - 8 * g), WIDTHS[g]), :])
            at = pl.ds(STARTS[g] + i * WIDTHS[g], WIDTHS[g])
            out_ref[at, :] = jnp.where(low_lanes((WIDTHS[g], 128)), rows[0], rows[1]) * first_ref[at, :]


def causal(rows, j):
    return lax.broadcasted_iota(jnp.int32, (rows, 256), 0) <= lax.broadcasted_iota(jnp.int32, (rows, 256), 1) + 256 * j


def local_kernel(kv_ref, q_ref, token_ref, out_ref, qt_ref):
    kv = kv_ref[...]
    k = kv[:, :DIM]
    vt = kv.astype(F32).T[DIM:].astype(BF16)
    qt_ref[...] = q_ref[...].astype(F32).T.astype(BF16)
    for hh in range(2):
        at = slice(hh * DIM, hh * DIM + DIM)
        for j in range(4):
            last = 256 * (j + 1)
            logits = dot(k[:last], qt_ref[at, 256 * j : last])
            w = jnp.where(causal(last, j), logits * logits * (1.0 / DIM), 0.0).astype(BF16)
            out_ref[at, 256 * j : last] = dot(vt[:, :last], w)


def ready_kernel(q_ref, g_ref, where_ref, before_ref, init_ref, second_ref, token_ref, out_ref, gt_out, base_out, x_ref):
    x_ref[...] = q_ref[...].astype(F32).T
    build_features(x_ref, DIM, out_ref, GROUP)
    gt_out[...] = g_ref[...].astype(F32).T
    core = where_ref[1].astype(F32)
    base_out[...] = init_ref[...] + second_ref[...] * (core * before_ref[...])


def key_feature_kernel(kv_ref, token_ref, out_ref, x_ref):
    x_ref[...] = kv_ref[...].astype(F32).T
    build_features(x_ref, 0, out_ref, GROUP)


def feature_kernel(hh, q_ref, token_ref, out_ref, x_ref, phi_ref, sems):
    x_ref[...] = q_ref[...].astype(F32).T
    copies = []
    for j in range(4):
        build_features(x_ref, DIM * hh, phi_ref, 256, 256 * j)
        lanes = pl.ds(256 * j, 256)
        copies.append(pltpu.make_async_copy(phi_ref.at[:, lanes], out_ref.at[:, lanes], sems.at[j]))
        copies[j].start()
    for copy in copies:
        copy.wait()


def sources(h):
    near = h + 1 - 2 * lax.rem(h, 2)
    return h, near, 3 - h, 3 - near


def place(where_ref, mine_ref, other_ref, out_ref):
    h, c = where_ref[0], where_ref[1]
    for s, source in enumerate(sources(h)):
        here = pl.ds(s * PIECE, PIECE)
        out_ref[pl.ds(pl.multiple_of((source * 2 + c) * PIECE, 8), PIECE), :] = mine_ref[here, :]
        out_ref[pl.ds(pl.multiple_of((source * 2 + 1 - c) * PIECE, 8), PIECE), :] = other_ref[here, :]


def flip_state(state, flat_ref):
    turned = state.T.astype(BF16)
    flat_ref[:, 0:ROWS] = turned[0:DIM]
    flat_ref[:, ROWS : 2 * ROWS] = turned[DIM : 2 * DIM]


def main_kernel(
    where_ref, mine_ref, other_ref, base_ref, second_hbm, g_ref, intra0_ref, intra1_ref, f0, f1, f2, f3,
    state_out, att_out, dn_out, g0, g1, g2, g3,
    sum_ref, flat_ref, gt_ref, grad_ref, phi_ref, sems, second_ref, more_sems,
):
    small = fetch([(second_hbm, second_ref)], more_sems)
    copies = [pltpu.make_async_copy(f, phi_ref.at[i], sems.at[i]) for i, f in enumerate((f0, f1, f2))]
    copies[0].start()
    place(where_ref, mine_ref, other_ref, sum_ref)
    small[0].wait()
    state = base_ref[...] + second_ref[...] * sum_ref[...]
    state_out[...] = state.astype(BF16)
    flip_state(state, flat_ref)
    order = (3, 0, 1, 2)
    copies[1].start()

    def features_of(step):
        return f3 if step == 0 else phi_ref.at[step - 1]

    def numer_of(step):
        hh = order[step]
        intra_ref = (intra0_ref, intra1_ref)[hh // 2]
        half = slice((hh % 2) * DIM, (hh % 2) * DIM + DIM)
        return dot(flat_ref[...], features_of(step)[...]) + intra_ref[half, :]

    following = numer_of(0)
    for step, hh in enumerate(order):
        at = slice(hh * DIM, hh * DIM + DIM)
        numer = following
        if step < 3:
            copies[step].wait()
            if step == 0:
                copies[2].start()
            following = numer_of(step + 1)
        scale = lax.rsqrt(jnp.mean(numer * numer, axis=0, keepdims=True) + EPSILON)
        y = numer * scale
        u = g_ref[at, :]
        dn = scale * (u - y * jnp.mean(u * y, axis=0, keepdims=True))
        gt_ref[at, :] = y
        dn_out[at, :] = dn.astype(BF16)
        twice = jnp.concatenate([dn, dn], axis=0).T.astype(BF16)
        feats = features_of(step)
        lo = dot(feats[0:ROWS], twice)
        hi = dot(feats[ROWS : 2 * ROWS], twice)
        total = jnp.where(low_lanes((ROWS, 128)), lo, hi)
        grad_ref[...] = total if step == 0 else grad_ref[...] + total
    for s, out in enumerate((g0, g1, g2, g3)):
        at = pl.multiple_of(lax.rem(where_ref[0] + s, 4) * 2 * PIECE, 8)
        out[...] = grad_ref[pl.ds(at, 2 * PIECE), :]
    att_out[...] = gt_ref[...].T.astype(BF16)


def back_local_kernel(kv_ref, q_ref, dn_ref, qg_out, kva_out, kvb_out, qt_ref, kvl_out):
    kv = kv_ref[...]
    k = kv[:, :DIM]
    v = kv[:, DIM:]
    kt = kv.astype(F32).T[:DIM].astype(BF16)
    qt_ref[...] = q_ref[...].astype(F32).T
    kvl_out[...] = jnp.zeros_like(kvl_out)
    low = low_lanes((256, 128))

    def head(hh, carry):
        at = pl.ds(pl.multiple_of(hh * DIM, DIM), DIM)
        for j in range(4):
            first, last = 256 * j, 256 * (j + 1)
            dnt = dn_ref[at, first:last]
            qt = qt_ref[at, first:last]
            logits = dot(k[:last], qt.astype(BF16))
            keep = causal(last, j)
            w = jnp.where(keep, logits * logits * (1.0 / DIM), 0.0).astype(BF16)
            dw = dot(v[:last], dnt)
            dl = jnp.where(keep, dw * logits * (2.0 / DIM), 0.0).astype(BF16)
            both = jnp.concatenate([qt, dnt.astype(F32)], axis=0).T.astype(BF16)
            qz = jnp.where(low, both, jnp.zeros_like(both))
            dnz = jnp.where(low, jnp.zeros_like(both), both)
            kvl_out[0:last, :] = kvl_out[0:last, :] + (dot(dl, qz) + dot(w, dnz))
            qg_out[at, first:last] = dot(kt[:, :last], dl)
        return carry

    lax.fori_loop(0, 4, head, 0)
    kva_out[...] = kvl_out[0 : GROUP // 2, :]
    kvb_out[...] = kvl_out[GROUP // 2 : GROUP, :]


def back_state_kernel(q_ref, dn_ref, state_ref, local_ref, *rest):
    out_ref, qt_ref, acc_ref, da_ref, db_ref, ra_ref, rb_ref = rest[-7:]
    qt_ref[...] = q_ref[...].astype(F32).T
    acc_ref[...] = local_ref[...]
    zeros = jnp.zeros((DIM, 256), BF16)

    def spread(hh, d_ref):
        dnt = dn_ref[hh * DIM : hh * DIM + DIM, :]
        d_ref[0:ROWS, :] = dot(state_ref[...], jnp.concatenate([dnt, zeros], axis=0))
        d_ref[ROWS : 2 * ROWS, :] = dot(state_ref[...], jnp.concatenate([zeros, dnt], axis=0))

    spread(0, da_ref)
    for hh in range(4):
        now, then = ((da_ref, db_ref), (db_ref, da_ref))[hh % 2]
        if hh < 3:
            spread(hh + 1, then)
        for step in range(2):
            fold_step(qt_ref, DIM * hh, 0, now, (ra_ref, rb_ref)[step], acc_ref, DIM * hh, 128 * step)
    out_ref[...] = acc_ref[...].T.astype(BF16)


def key_kernel(
    where_ref, part_ref, before_ref, after_ref, across_a_ref, across_b_ref, second_ref, x_ref,
    kv_a_ref, kv_b_ref, got_a_ref, got_b_ref, phi_ref,
    out_ref,
    sum_ref, low_ref, flat_ref, acc_ref, da_ref, db_ref, ra_ref, rb_ref,
):
    for s, refs in enumerate(((part_ref,), (after_ref,), (across_a_ref, across_b_ref), (before_ref,))):
        at = lax.rem(where_ref[0] + s, 4) * 2 * PIECE
        for i, ref in enumerate(refs):
            rows = 2 * PIECE // len(refs)
            sum_ref[pl.ds(pl.multiple_of(at + i * rows, 8), rows), :] = ref[...]
    state = second_ref[...] * sum_ref[...]
    low_ref[...] = state.astype(BF16)
    flip_state(state, flat_ref)
    acc_ref[0:DIM, :] = jnp.zeros((DIM, GROUP), F32)
    zeros = jnp.zeros((DIM, 256), BF16)

    def spread(j, d_ref):
        vt = x_ref[DIM : 2 * DIM, 256 * j : 256 * j + 256].astype(BF16)
        d_ref[0:ROWS, :] = dot(low_ref[...], jnp.concatenate([vt, zeros], axis=0))
        d_ref[ROWS : 2 * ROWS, :] = dot(low_ref[...], jnp.concatenate([zeros, vt], axis=0))

    spread(0, da_ref)
    for j in range(4):
        now, then = ((da_ref, db_ref), (db_ref, da_ref))[j % 2]
        if j < 3:
            spread(j + 1, then)
        else:
            acc_ref[DIM : 2 * DIM, :] = dot(flat_ref[...], phi_ref[...])
        for step in range(2):
            fold_step(x_ref, 0, 256 * j, now, (ra_ref, rb_ref)[step], acc_ref, 0, 128 * step)
    turned = acc_ref[...].T
    out_ref[0 : GROUP // 2, :] = (kv_a_ref[...] + got_a_ref[...]) + turned[0 : GROUP // 2]
    out_ref[GROUP // 2 : GROUP, :] = (kv_b_ref[...] + got_b_ref[...]) + turned[GROUP // 2 : GROUP]


LOW, HIGH = 96, 48


def total_kernel(where_ref, own_ref, low_ref, high_ref, first_ref, out_ref, sum_ref, t_ref):
    width = FEATURES // 4
    for part in range(4):

        @pl.when(where_ref[0] == part)
        def _(part=part, first=part * width, last=(part + 1) * width):
            start = part * 2 * PIECE
            sum_ref[start : start + 2 * PIECE, :] = own_ref[...]
            if part > 0:
                sum_ref[start - LOW : start, :] = low_ref[...]
            if part < 3:
                sum_ref[start + 2 * PIECE : start + 2 * PIECE + HIGH, :] = high_ref[...]
            for a in reversed(range(DIM)):
                if triu_start(a) >= last or triu_start(a + 1) <= first:
                    continue
                g = a // 8
                at = pl.ds(STARTS[g] + (a % 4) * WIDTHS[g], WIDTHS[g])
                piece = sum_ref[at, :] * first_ref[at, :]
                if a % 8 >= 4:
                    piece = pltpu.roll(piece, 64, 1)
                t_ref[pl.ds(triu_start(a) - (a - 8 * g), WIDTHS[g]), :] = piece
            out_ref[...] = t_ref[first:last, :].T[0:DIM]


def vmem(shape, kind=F32):
    return pltpu.VMEM(shape, kind)


WHOLE = pl.BlockSpec(memory_space=pltpu.VMEM)
SCALAR = pl.BlockSpec(memory_space=pltpu.SMEM)
LEFT = pl.BlockSpec(memory_space=pltpu.HBM)


def block(shape, at):
    return pl.BlockSpec(shape, lambda i: at)


def call(kernel, outs, scratch, args, specs=None, out_specs=None, grid=(), aliases=None, limit=40):
    specs = specs or [WHOLE] * len(args)
    out_specs = out_specs or [WHOLE] * len(outs)
    args = [pltpu.with_memory_space_constraint(a, pltpu.HBM) if s is LEFT else a for a, s in zip(args, specs)]
    return pl.pallas_call(
        kernel,
        grid=grid,
        out_shape=[pltpu.HBM(s, k) if o is LEFT else jax.ShapeDtypeStruct(s, k) for (s, k), o in zip(outs, out_specs)],
        in_specs=specs,
        out_specs=out_specs,
        scratch_shapes=scratch,
        input_output_aliases=aliases or {},
        compiler_params=pltpu.CompilerParams(vmem_limit_bytes=limit * MIB),
    )(*args)


PAIRS = {
    "c": lambda x, y, z, c: (x, y, z, 1 - c),
    "z0": lambda x, y, z, c: (x, y, z ^ 1, c),
    "z1": lambda x, y, z, c: (x, y, 3 - z, c),
    "y0": lambda x, y, z, c: (x, y ^ 1, z, c),
    "y1": lambda x, y, z, c: (x, 3 - y, z, c),
}


def move(x, step):
    if step in PAIRS:
        pairs = []
        for j in range(32):
            _, y, z, c = PAIRS[step](0, j // 8, (j // 2) % 4, j % 2)
            pairs.append((j, y * 8 + z * 2 + c))
        return lax.ppermute(x, "seq", pairs)
    if step == "x0":
        return lax.ppermute(x, "head", [(j, j ^ 1) for j in range(4)])
    if step == "x1":
        return lax.ppermute(x, "head", [(j, 3 - j) for j in range(4)])
    return lax.ppermute(x, "head", [(j, (j + step) % 4) for j in range(4)])


def take(x, index, rows):
    return lax.dynamic_slice_in_dim(x, index * rows, rows, 0)


def tie(x, *others):
    return lax.optimization_barrier((x,) + others)[0]


def per_device(queries, keys_values, init_state, out_grad):
    h = lax.axis_index("head")
    seq = lax.axis_index("seq")
    c, z, y = seq % 2, (seq // 2) % 4, seq // 8
    where = jnp.stack([h, c]).astype(jnp.int32)
    first, second = jnp.asarray(FIRST), jnp.asarray(SECOND)
    half = h * 2 + c

    def features_of(hh, token):
        return call(
            functools.partial(feature_kernel, hh % 2),
            [((2 * ROWS, GROUP), BF16)],
            [vmem((128, GROUP)), vmem((2 * ROWS, GROUP), BF16), pltpu.SemaphoreType.DMA((4,))],
            [queries, token],
            specs=[block((GROUP, 128), (0, hh // 2)), block((8, 128), (0, 0))],
            out_specs=[LEFT],
            grid=(1,),
            limit=10,
        )[0]

    def ready_of(token):
        token_block = block((8, 128), (0, 0))
        shapes = [((2 * ROWS, GROUP), BF16), ((4 * DIM, GROUP), F32), ((ROWS, 128), F32)]
        return call(
            ready_kernel,
            shapes,
            [vmem((128, GROUP))],
            [queries, out_grad, where, other_update, init_low, second, token],
            specs=[block((GROUP, 128), (0, 1)), WHOLE, SCALAR, WHOLE, WHOLE, WHOLE, token_block],
            out_specs=[block(shape, (0, 0)) for shape, _ in shapes],
            grid=(1,),
            limit=16,
        )

    def local_of(p, token):
        return call(
            local_kernel,
            [((128, GROUP), F32)],
            [vmem((128, GROUP), BF16)],
            [keys_values, queries, token],
            specs=[WHOLE, block((GROUP, 128), (0, p)), block((8, 128), (0, 0))],
            out_specs=[block((128, GROUP), (0, 0))],
            grid=(1,),
            limit=10,
        )[0]

    (update,) = call(
        update_kernel,
        [((ROWS, 128), F32)],
        [
            vmem((128, GROUP)), vmem((2 * ROWS, GROUP), BF16), vmem((GROUP, 128), BF16), pltpu.SemaphoreType.DMA((1,)),
        ],
        [keys_values],
        specs=[LEFT],
        limit=12,
    )
    (init_low,) = call(
        init_kernel,
        [((ROWS, 128), F32)],
        [
            vmem((FEATURES, 128)), vmem((DIM, FEATURES)), vmem((ROWS, 128)), pltpu.SemaphoreType.DMA((2,)),
        ],
        [tie(init_state, update), first],
        specs=[LEFT, LEFT],
        limit=8,
    )
    other_update = move(update, "c")
    chip = take(update, half, PIECE) + take(other_update, half, PIECE)
    chip = tie(chip, init_low)
    feats = [None] * 4
    feats[0] = features_of(0, chip)
    got = move(chip, "z0")
    part = jnp.where(z % 2 == 1, got, 0.0)
    total = tie(chip + got, feats[0])
    feats[1] = features_of(1, total)
    got = move(total, "z1")
    part = part + jnp.where(z >= 2, got, 0.0)
    total = tie(total + got, feats[1])
    feats[2] = features_of(2, total)
    got = move(total, "y0")
    part = part + jnp.where(y % 2 == 1, got, 0.0)
    total = tie(total + got, feats[2])
    intra0 = local_of(0, total)
    got = move(total, "y1")
    part = tie(part + jnp.where(y >= 2, got, 0.0), intra0)
    intra1 = local_of(1, part)
    stack = jnp.concatenate([part, move(part, "x0")], axis=0)
    stack = tie(stack, intra1)
    feats[3], turned_grad, base = ready_of(stack)
    stack = jnp.concatenate([stack, move(stack, "x1")], axis=0)
    stack = tie(stack, feats[3])
    other = move(stack, "c")

    state, attended, dn, mine, *sends = call(
        main_kernel,
        [((ROWS, 128), BF16), ((GROUP, 4 * DIM), BF16), ((4 * DIM, GROUP), BF16)] + [((2 * PIECE, 128), F32)] * 4,
        [
            vmem((ROWS, 128)),
            vmem((DIM, 2 * ROWS), BF16),
            vmem((4 * DIM, GROUP)),
            vmem((ROWS, 128)),
            vmem((3, 2 * ROWS, GROUP), BF16),
            pltpu.SemaphoreType.DMA((3,)),
            vmem((ROWS, 128)),
            pltpu.SemaphoreType.DMA((1,)),
        ],
        [where, stack, other, base, second, turned_grad, intra0, intra1] + feats,
        specs=[SCALAR] + [WHOLE] * 3 + [LEFT] + [WHOLE] * 3 + [LEFT] * 3 + [WHOLE],
        limit=30,
    )

    qg_local, kv_a, kv_b = call(
        back_local_kernel,
        [((4 * DIM, GROUP), F32), ((GROUP // 2, 128), F32), ((GROUP // 2, 128), F32)],
        [vmem((4 * DIM, GROUP)), vmem((GROUP, 128))],
        [keys_values, queries, dn],
        limit=16,
    )
    own = mine + move(sends[0], 1) + move(sends[1], 2) + move(sends[2], 3)
    own = tie(own, kv_a)
    other_own = move(own, "c")
    chip = own + other_own
    core_grad = jnp.where(c == 0, other_own, 0.0)

    def state_part(j, dn, before):
        extra = [] if before is None else [before]
        return call(
            back_state_kernel,
            [((GROUP, 4 * DIM), BF16)],
            [vmem((4 * DIM, 256))] * 2 + [vmem((2 * ROWS, 256))] * 2 + [vmem((DIM, 128))] * 2,
            [queries, dn, state, qg_local] + extra,
            specs=[block((256, 256), (j, 0)), block((256, 256), (0, j)), WHOLE, block((256, 256), (0, j))]
            + [LEFT] * len(extra),
            out_specs=[block((256, 256), (j, 0))],
            grid=(1,),
            aliases={4: 0} if extra else None,
            limit=12,
        )[0]

    got = move(chip, "z0")
    got_a, got_b = move(kv_a, "x0"), move(kv_b, "x1")
    qg = state_part(0, tie(dn, chip), None)
    part = core_grad + jnp.where(z % 2 == 0, got, 0.0)
    total = tie(chip + got, qg)

    got = move(total, "z1")
    qg = state_part(1, tie(dn, total), qg)
    part = part + jnp.where(z < 2, got, 0.0)
    kv_a = tie(kv_a, qg) + got_a
    kv_b = tie(kv_b, qg) + got_b
    total = tie(total + got, qg, kv_a, kv_b)

    got = move(total, "y0")
    got_a, got_b = move(tie(kv_a, total), "x1"), move(tie(kv_b, total), "x0")
    qg = state_part(2, tie(dn, total), qg)
    part = part + jnp.where(y % 2 == 0, got, 0.0)
    total = tie(total + got, qg)

    got = move(total, "y1")
    qg = state_part(3, tie(dn, total, got_a, got_b), qg)
    part = tie(part + jnp.where(y < 2, got, 0.0), qg)
    every = total + got

    before, after = move(part, 1), move(part, 3)
    key_feats, turned_kv = call(
        key_feature_kernel,
        [((2 * ROWS, GROUP), BF16), ((128, GROUP), F32)],
        [],
        [keys_values, part],
        specs=[block((GROUP, 128), (0, 0)), block((8, 128), (0, 0))],
        out_specs=[block((2 * ROWS, GROUP), (0, 0)), block((128, GROUP), (0, 0))],
        grid=(1,),
        limit=12,
    )
    every_low, every_high = move(every[2 * PIECE - LOW :], 1), move(every[:HIGH], 3)
    before, after = tie(before, key_feats, every_low), tie(after, key_feats, every_high)
    across_a, across_b = move(after[:PIECE], 3), move(before[PIECE:], 1)

    (kv_grad,) = call(
        key_kernel,
        [((GROUP, 128), F32)],
        [vmem((ROWS, 128)), vmem((ROWS, 128), BF16), vmem((DIM, 2 * ROWS), BF16), vmem((128, GROUP))]
        + [vmem((2 * ROWS, 256))] * 2
        + [vmem((DIM, 128))] * 2,
        [where, part, before, after, across_a, across_b, second, turned_kv, kv_a, kv_b, got_a, got_b, key_feats],
        specs=[SCALAR] + [WHOLE] * 12,
        limit=20,
    )
    (init_grad,) = call(
        total_kernel,
        [((DIM, FEATURES // 4), F32)],
        [vmem((ROWS, 128)), vmem((FEATURES, 128))],
        [where, every, tie(every_low, kv_grad), every_high, first],
        specs=[SCALAR] + [WHOLE] * 4,
        limit=8,
    )
    return attended, qg, kv_grad, init_grad


def solution(mesh):
    return jax.shard_map(
        per_device,
        mesh=mesh,
        in_specs=(P("seq", "head"), P("seq", None), P(), P("seq", "head")),
        out_specs=(P("seq", "head"), P("seq", "head"), P("seq", None), P(None, "head")),
        check_vma=False,
    )
```

```python
import functools

import jax
import jax.numpy as jnp
import numpy as np
from jax import lax
from jax.experimental import pallas as pl
from jax.experimental.pallas import tpu as pltpu
from jax.sharding import PartitionSpec as P

DIM = 64
GROUP = 1024
FEATURES = 2080
EPSILON = 1e-06
WIDTHS = [DIM - 8 * g for g in range(8)]
STARTS = [sum(4 * w for w in WIDTHS[:g]) for g in range(8)]
ROWS = sum(4 * w for w in WIDTHS)
PIECE = ROWS // 8
F32 = jnp.float32
BF16 = jnp.bfloat16
MIB = 1024 * 1024


def weights_of():
    c = np.zeros((ROWS, 128), np.float32)
    for g in range(8):
        for half in range(2):
            for i in range(4):
                a = 8 * g + 4 * half + i
                b = np.arange(8 * g, DIM)
                value = np.where(b == a, 1.0, np.where(b > a, np.sqrt(2.0), 0.0)) / np.sqrt(DIM)
                row = STARTS[g] + i * WIDTHS[g]
                c[row : row + WIDTHS[g], 64 * half : 64 * half + 64] = value[:, None]
    return c


FIRST = weights_of()
SECOND = np.where(FIRST > 0, np.where(FIRST > 0.15, 2.0 / DIM, 1.0 / DIM), 0.0).astype(np.float32)


def triu_start(a):
    return DIM * a - a * (a - 1) // 2


def dot(x, y):
    return lax.dot_general(x, y, (((1,), (0,)), ((), ())), preferred_element_type=F32)


def build_step(x_ref, base, phi_ref, lanes):
    for g in range(8):
        tail = x_ref[pl.ds(base + 8 * g, WIDTHS[g]), lanes]
        for half in range(2):
            parts = []
            for i in range(4):
                a = 8 * g + 4 * half + i
                parts.append(tail[a - 8 * g : a - 8 * g + 1, :] * tail)
            block = jnp.concatenate(parts, axis=0).astype(BF16)
            phi_ref[pl.ds(half * ROWS + STARTS[g], 4 * WIDTHS[g]), lanes] = block


def build_features(x_ref, base, phi_ref, tokens, start=0):
    def one(step, carry):
        build_step(x_ref, base, phi_ref, pl.ds(pl.multiple_of(start + step * 128, 128), 128))
        return carry

    lax.fori_loop(0, tokens // 128, one, 0)


def fold_step(x_ref, base, x_lane, d_ref, rows_ref, out_ref, out_base, at):
    lanes = pl.ds(at, 128)
    xl = pl.ds(x_lane + at, 128)
    x = x_ref[pl.ds(base, DIM), xl]
    acc = [jnp.zeros((8, 128), F32) for _ in range(8)]
    for g in range(8):
        for half in range(2):
            for i in range(4):
                a = 8 * g + 4 * half + i
                xa = x[a : a + 1, :]
                row = half * ROWS + STARTS[g] + i * WIDTHS[g]
                total = None
                for k in range(g, 8):
                    d = d_ref[pl.ds(row + 8 * (k - g), 8), lanes]
                    acc[k] = acc[k] + d * xa
                    term = d * x[8 * k : 8 * k + 8, :]
                    total = term if total is None else total + term
                rows_ref[a : a + 1, :] = jnp.sum(total, axis=0, keepdims=True)
    grad = jnp.concatenate(acc, axis=0) + rows_ref[...]
    out_ref[pl.ds(out_base, DIM), xl] = out_ref[pl.ds(out_base, DIM), xl] + grad


def low_lanes(shape):
    return lax.broadcasted_iota(jnp.int32, shape, 1) < 64


def update_kernel(kv_hbm, out_ref, x_ref, phi_ref, kv_ref, sems):
    fetch([(kv_hbm, kv_ref)], sems)[0].wait()
    kv = kv_ref[...]
    x_ref[...] = kv.astype(F32).T
    v = kv[:, DIM:]
    vv = jnp.concatenate([v, v], axis=1)
    low = low_lanes((ROWS, 128))
    for j in range(4):
        tokens = slice(256 * j, 256 * j + 256)
        for at in (256 * j, 256 * j + 128):
            build_step(x_ref, 0, phi_ref, pl.ds(at, 128))
        lo = dot(phi_ref[0:ROWS, tokens], vv[tokens])
        hi = dot(phi_ref[ROWS : 2 * ROWS, tokens], vv[tokens])
        part = jnp.where(low, lo, hi)
        out_ref[...] = part if j == 0 else out_ref[...] + part


def fetch(pairs, sems):
    copies = [pltpu.make_async_copy(a, b, sems.at[i]) for i, (a, b) in enumerate(pairs)]
    for copy in copies:
        copy.start()
    return copies


def init_kernel(init_hbm, first_hbm, out_ref, t_ref, init_ref, first_ref, sems):
    for copy in fetch([(init_hbm, init_ref), (first_hbm, first_ref)], sems):
        copy.wait()
    t_ref[...] = jnp.concatenate([init_ref[...], init_ref[...]], axis=0).T
    for g in range(8):
        for i in range(4):
            rows = []
            for half in range(2):
                a = 8 * g + 4 * half + i
                rows.append(t_ref[pl.ds(triu_start(a) - (a - 8 * g), WIDTHS[g]), :])
            at = pl.ds(STARTS[g] + i * WIDTHS[g], WIDTHS[g])
            out_ref[at, :] = jnp.where(low_lanes((WIDTHS[g], 128)), rows[0], rows[1]) * first_ref[at, :]


def causal(rows, j):
    return lax.broadcasted_iota(jnp.int32, (rows, 256), 0) <= lax.broadcasted_iota(jnp.int32, (rows, 256), 1) + 256 * j


def local_kernel(kv_ref, q_ref, token_ref, out_ref, qt_ref):
    kv = kv_ref[...]
    k = kv[:, :DIM]
    vt = kv.astype(F32).T[DIM:].astype(BF16)
    qt_ref[...] = q_ref[...].astype(F32).T.astype(BF16)
    for hh in range(2):
        at = slice(hh * DIM, hh * DIM + DIM)
        for j in range(4):
            last = 256 * (j + 1)
            logits = dot(k[:last], qt_ref[at, 256 * j : last])
            w = jnp.where(causal(last, j), logits * logits * (1.0 / DIM), 0.0).astype(BF16)
            out_ref[at, 256 * j : last] = dot(vt[:, :last], w)


def ready_kernel(q_ref, g_ref, where_ref, before_ref, init_ref, second_ref, token_ref, out_ref, gt_out, base_out, x_ref):
    x_ref[...] = q_ref[...].astype(F32).T
    build_features(x_ref, DIM, out_ref, GROUP)
    gt_out[...] = g_ref[...].astype(F32).T
    core = where_ref[1].astype(F32)
    base_out[...] = init_ref[...] + second_ref[...] * (core * before_ref[...])


def key_feature_kernel(kv_ref, token_ref, out_ref, x_ref):
    x_ref[...] = kv_ref[...].astype(F32).T
    build_features(x_ref, 0, out_ref, GROUP)


def first_feature_kernel(q_hbm, token_ref, out_ref, x_ref, phi_ref, sems, q_ref, q_sems):
    fetch([(q_hbm.at[:, 0:128], q_ref)], q_sems)[0].wait()
    feature_kernel(0, q_ref, token_ref, out_ref, x_ref, phi_ref, sems)


def feature_kernel(hh, q_ref, token_ref, out_ref, x_ref, phi_ref, sems):
    x_ref[...] = q_ref[...].astype(F32).T
    copies = []
    for j in range(4):
        build_features(x_ref, DIM * hh, phi_ref, 256, 256 * j)
        lanes = pl.ds(256 * j, 256)
        copies.append(pltpu.make_async_copy(phi_ref.at[:, lanes], out_ref.at[:, lanes], sems.at[j]))
        copies[j].start()
    for copy in copies:
        copy.wait()


def sources(h):
    near = h + 1 - 2 * lax.rem(h, 2)
    return h, near, 3 - h, 3 - near


def place(where_ref, mine_ref, other_ref, out_ref):
    h, c = where_ref[0], where_ref[1]
    for s, source in enumerate(sources(h)):
        here = pl.ds(s * PIECE, PIECE)
        out_ref[pl.ds(pl.multiple_of((source * 2 + c) * PIECE, 8), PIECE), :] = mine_ref[here, :]
        out_ref[pl.ds(pl.multiple_of((source * 2 + 1 - c) * PIECE, 8), PIECE), :] = other_ref[here, :]


def flip_state(state, flat_ref):
    turned = state.T.astype(BF16)
    flat_ref[:, 0:ROWS] = turned[0:DIM]
    flat_ref[:, ROWS : 2 * ROWS] = turned[DIM : 2 * DIM]


def main_kernel(
    where_ref, mine_ref, other_ref, base_ref, second_hbm, g_ref, intra0_ref, intra1_ref, f0, f1, f2, f3,
    state_out, att_out, dn_out, g0, g1, g2, g3,
    sum_ref, flat_ref, gt_ref, grad_ref, phi_ref, sems, second_ref, more_sems,
):
    small = fetch([(second_hbm, second_ref)], more_sems)
    copies = [pltpu.make_async_copy(f, phi_ref.at[i], sems.at[i]) for i, f in enumerate((f0, f1, f2))]
    copies[0].start()
    place(where_ref, mine_ref, other_ref, sum_ref)
    small[0].wait()
    state = base_ref[...] + second_ref[...] * sum_ref[...]
    state_out[...] = state.astype(BF16)
    flip_state(state, flat_ref)
    order = (3, 0, 1, 2)
    copies[1].start()

    def features_of(step):
        return f3 if step == 0 else phi_ref.at[step - 1]

    def numer_of(step):
        hh = order[step]
        intra_ref = (intra0_ref, intra1_ref)[hh // 2]
        half = slice((hh % 2) * DIM, (hh % 2) * DIM + DIM)
        return dot(flat_ref[...], features_of(step)[...]) + intra_ref[half, :]

    following = numer_of(0)
    for step, hh in enumerate(order):
        at = slice(hh * DIM, hh * DIM + DIM)
        numer = following
        if step < 3:
            copies[step].wait()
            if step == 0:
                copies[2].start()
            following = numer_of(step + 1)
        scale = lax.rsqrt(jnp.mean(numer * numer, axis=0, keepdims=True) + EPSILON)
        y = numer * scale
        u = g_ref[at, :]
        dn = scale * (u - y * jnp.mean(u * y, axis=0, keepdims=True))
        gt_ref[at, :] = y
        dn_out[at, :] = dn.astype(BF16)
        twice = jnp.concatenate([dn, dn], axis=0).T.astype(BF16)
        feats = features_of(step)
        lo = dot(feats[0:ROWS], twice)
        hi = dot(feats[ROWS : 2 * ROWS], twice)
        total = jnp.where(low_lanes((ROWS, 128)), lo, hi)
        grad_ref[...] = total if step == 0 else grad_ref[...] + total
    for s, out in enumerate((g0, g1, g2, g3)):
        at = pl.multiple_of(lax.rem(where_ref[0] + s, 4) * 2 * PIECE, 8)
        out[...] = grad_ref[pl.ds(at, 2 * PIECE), :]
    att_out[...] = gt_ref[...].T.astype(BF16)


def back_local_kernel(kv_ref, q_ref, dn_ref, qg_out, kva_out, kvb_out, qt_ref, kvl_out):
    kv = kv_ref[...]
    k = kv[:, :DIM]
    v = kv[:, DIM:]
    kt = kv.astype(F32).T[:DIM].astype(BF16)
    qt_ref[...] = q_ref[...].astype(F32).T
    kvl_out[...] = jnp.zeros_like(kvl_out)
    low = low_lanes((256, 128))

    def head(hh, carry):
        at = pl.ds(pl.multiple_of(hh * DIM, DIM), DIM)
        for j in range(4):
            first, last = 256 * j, 256 * (j + 1)
            dnt = dn_ref[at, first:last]
            qt = qt_ref[at, first:last]
            logits = dot(k[:last], qt.astype(BF16))
            keep = causal(last, j)
            w = jnp.where(keep, logits * logits * (1.0 / DIM), 0.0).astype(BF16)
            dw = dot(v[:last], dnt)
            dl = jnp.where(keep, dw * logits * (2.0 / DIM), 0.0).astype(BF16)
            both = jnp.concatenate([qt, dnt.astype(F32)], axis=0).T.astype(BF16)
            qz = jnp.where(low, both, jnp.zeros_like(both))
            dnz = jnp.where(low, jnp.zeros_like(both), both)
            kvl_out[0:last, :] = kvl_out[0:last, :] + (dot(dl, qz) + dot(w, dnz))
            qg_out[at, first:last] = dot(kt[:, :last], dl)
        return carry

    lax.fori_loop(0, 4, head, 0)
    kva_out[...] = kvl_out[0 : GROUP // 2, :]
    kvb_out[...] = kvl_out[GROUP // 2 : GROUP, :]


def back_state_kernel(q_ref, dn_ref, state_ref, local_ref, *rest):
    out_ref, qt_ref, acc_ref, da_ref, db_ref, ra_ref, rb_ref = rest[-7:]
    qt_ref[...] = q_ref[...].astype(F32).T
    acc_ref[...] = local_ref[...]
    zeros = jnp.zeros((DIM, 256), BF16)

    def spread(hh, d_ref):
        dnt = dn_ref[hh * DIM : hh * DIM + DIM, :]
        d_ref[0:ROWS, :] = dot(state_ref[...], jnp.concatenate([dnt, zeros], axis=0))
        d_ref[ROWS : 2 * ROWS, :] = dot(state_ref[...], jnp.concatenate([zeros, dnt], axis=0))

    spread(0, da_ref)
    for hh in range(4):
        now, then = ((da_ref, db_ref), (db_ref, da_ref))[hh % 2]
        if hh < 3:
            spread(hh + 1, then)
        for step in range(2):
            fold_step(qt_ref, DIM * hh, 0, now, (ra_ref, rb_ref)[step], acc_ref, DIM * hh, 128 * step)
    out_ref[...] = acc_ref[...].T.astype(BF16)


def key_kernel(
    where_ref, part_ref, before_ref, after_ref, across_a_ref, across_b_ref, second_ref, x_ref,
    kv_a_ref, kv_b_ref, got_a_ref, got_b_ref, phi_ref,
    out_ref,
    sum_ref, low_ref, flat_ref, acc_ref, da_ref, db_ref, ra_ref, rb_ref,
):
    for s, refs in enumerate(((part_ref,), (after_ref,), (across_a_ref, across_b_ref), (before_ref,))):
        at = lax.rem(where_ref[0] + s, 4) * 2 * PIECE
        for i, ref in enumerate(refs):
            rows = 2 * PIECE // len(refs)
            sum_ref[pl.ds(pl.multiple_of(at + i * rows, 8), rows), :] = ref[...]
    state = second_ref[...] * sum_ref[...]
    low_ref[...] = state.astype(BF16)
    flip_state(state, flat_ref)
    acc_ref[0:DIM, :] = jnp.zeros((DIM, GROUP), F32)
    zeros = jnp.zeros((DIM, 256), BF16)

    def spread(j, d_ref):
        vt = x_ref[DIM : 2 * DIM, 256 * j : 256 * j + 256].astype(BF16)
        d_ref[0:ROWS, :] = dot(low_ref[...], jnp.concatenate([vt, zeros], axis=0))
        d_ref[ROWS : 2 * ROWS, :] = dot(low_ref[...], jnp.concatenate([zeros, vt], axis=0))

    spread(0, da_ref)
    for j in range(4):
        now, then = ((da_ref, db_ref), (db_ref, da_ref))[j % 2]
        if j < 3:
            spread(j + 1, then)
        else:
            acc_ref[DIM : 2 * DIM, :] = dot(flat_ref[...], phi_ref[...])
        for step in range(2):
            fold_step(x_ref, 0, 256 * j, now, (ra_ref, rb_ref)[step], acc_ref, 0, 128 * step)
    turned = acc_ref[...].T
    out_ref[0 : GROUP // 2, :] = (kv_a_ref[...] + got_a_ref[...]) + turned[0 : GROUP // 2]
    out_ref[GROUP // 2 : GROUP, :] = (kv_b_ref[...] + got_b_ref[...]) + turned[GROUP // 2 : GROUP]


LOW, HIGH = 96, 48


def total_kernel(where_ref, own_ref, low_ref, high_ref, first_ref, out_ref, sum_ref, t_ref):
    width = FEATURES // 4
    for part in range(4):

        @pl.when(where_ref[0] == part)
        def _(part=part, first=part * width, last=(part + 1) * width):
            start = part * 2 * PIECE
            sum_ref[start : start + 2 * PIECE, :] = own_ref[...]
            if part > 0:
                sum_ref[start - LOW : start, :] = low_ref[...]
            if part < 3:
                sum_ref[start + 2 * PIECE : start + 2 * PIECE + HIGH, :] = high_ref[...]
            for a in reversed(range(DIM)):
                if triu_start(a) >= last or triu_start(a + 1) <= first:
                    continue
                g = a // 8
                at = pl.ds(STARTS[g] + (a % 4) * WIDTHS[g], WIDTHS[g])
                piece = sum_ref[at, :] * first_ref[at, :]
                if a % 8 >= 4:
                    piece = pltpu.roll(piece, 64, 1)
                t_ref[pl.ds(triu_start(a) - (a - 8 * g), WIDTHS[g]), :] = piece
            out_ref[...] = t_ref[first:last, :].T[0:DIM]


def vmem(shape, kind=F32):
    return pltpu.VMEM(shape, kind)


WHOLE = pl.BlockSpec(memory_space=pltpu.VMEM)
SCALAR = pl.BlockSpec(memory_space=pltpu.SMEM)
LEFT = pl.BlockSpec(memory_space=pltpu.HBM)


def block(shape, at):
    return pl.BlockSpec(shape, lambda i: at)


def call(kernel, outs, scratch, args, specs=None, out_specs=None, grid=(), aliases=None, limit=40):
    specs = specs or [WHOLE] * len(args)
    out_specs = out_specs or [WHOLE] * len(outs)
    args = [pltpu.with_memory_space_constraint(a, pltpu.HBM) if s is LEFT else a for a, s in zip(args, specs)]
    return pl.pallas_call(
        kernel,
        grid=grid,
        out_shape=[pltpu.HBM(s, k) if o is LEFT else jax.ShapeDtypeStruct(s, k) for (s, k), o in zip(outs, out_specs)],
        in_specs=specs,
        out_specs=out_specs,
        scratch_shapes=scratch,
        input_output_aliases=aliases or {},
        compiler_params=pltpu.CompilerParams(vmem_limit_bytes=limit * MIB),
    )(*args)


PAIRS = {
    "c": lambda x, y, z, c: (x, y, z, 1 - c),
    "z0": lambda x, y, z, c: (x, y, z ^ 1, c),
    "z1": lambda x, y, z, c: (x, y, 3 - z, c),
    "y0": lambda x, y, z, c: (x, y ^ 1, z, c),
    "y1": lambda x, y, z, c: (x, 3 - y, z, c),
}


def move(x, step):
    if step in PAIRS:
        pairs = []
        for j in range(32):
            _, y, z, c = PAIRS[step](0, j // 8, (j // 2) % 4, j % 2)
            pairs.append((j, y * 8 + z * 2 + c))
        return lax.ppermute(x, "seq", pairs)
    if step == "x0":
        return lax.ppermute(x, "head", [(j, j ^ 1) for j in range(4)])
    if step == "x1":
        return lax.ppermute(x, "head", [(j, 3 - j) for j in range(4)])
    return lax.ppermute(x, "head", [(j, (j + step) % 4) for j in range(4)])


def take(x, index, rows):
    return lax.dynamic_slice_in_dim(x, index * rows, rows, 0)


def tie(x, *others):
    return lax.optimization_barrier((x,) + others)[0]


def per_device(queries, keys_values, init_state, out_grad):
    h = lax.axis_index("head")
    seq = lax.axis_index("seq")
    c, z, y = seq % 2, (seq // 2) % 4, seq // 8
    where = jnp.stack([h, c]).astype(jnp.int32)
    first, second = jnp.asarray(FIRST), jnp.asarray(SECOND)
    half = h * 2 + c

    def features_of(hh, token):
        more = [vmem((GROUP, 128), BF16), pltpu.SemaphoreType.DMA((1,))] if hh == 0 else []
        return call(
            functools.partial(feature_kernel, hh % 2) if hh else first_feature_kernel,
            [((2 * ROWS, GROUP), BF16)],
            [vmem((128, GROUP)), vmem((2 * ROWS, GROUP), BF16), pltpu.SemaphoreType.DMA((4,))] + more,
            [queries, token],
            specs=[block((GROUP, 128), (0, hh // 2)) if hh else LEFT, block((8, 128), (0, 0))],
            out_specs=[LEFT],
            grid=(1,),
            limit=10,
        )[0]

    def ready_of(token):
        token_block = block((8, 128), (0, 0))
        shapes = [((2 * ROWS, GROUP), BF16), ((4 * DIM, GROUP), F32), ((ROWS, 128), F32)]
        return call(
            ready_kernel,
            shapes,
            [vmem((128, GROUP))],
            [queries, out_grad, where, other_update, init_low, second, token],
            specs=[block((GROUP, 128), (0, 1)), WHOLE, SCALAR, WHOLE, WHOLE, WHOLE, token_block],
            out_specs=[block(shape, (0, 0)) for shape, _ in shapes],
            grid=(1,),
            limit=16,
        )

    def local_of(p, token):
        return call(
            local_kernel,
            [((128, GROUP), F32)],
            [vmem((128, GROUP), BF16)],
            [keys_values, queries, token],
            specs=[WHOLE, block((GROUP, 128), (0, p)), block((8, 128), (0, 0))],
            out_specs=[block((128, GROUP), (0, 0))],
            grid=(1,),
            limit=10,
        )[0]

    (update,) = call(
        update_kernel,
        [((ROWS, 128), F32)],
        [
            vmem((128, GROUP)), vmem((2 * ROWS, GROUP), BF16), vmem((GROUP, 128), BF16), pltpu.SemaphoreType.DMA((1,)),
        ],
        [keys_values],
        specs=[LEFT],
        limit=12,
    )
    (init_low,) = call(
        init_kernel,
        [((ROWS, 128), F32)],
        [
            vmem((FEATURES, 128)), vmem((DIM, FEATURES)), vmem((ROWS, 128)), pltpu.SemaphoreType.DMA((2,)),
        ],
        [tie(init_state, update), first],
        specs=[LEFT, LEFT],
        limit=8,
    )
    other_update = move(update, "c")
    chip = take(update, half, PIECE) + take(other_update, half, PIECE)
    chip = tie(chip, init_low)
    feats = [None] * 4
    feats[0] = features_of(0, chip)
    got = move(chip, "z0")
    part = jnp.where(z % 2 == 1, got, 0.0)
    total = tie(chip + got, feats[0])
    feats[1] = features_of(1, total)
    got = move(total, "z1")
    part = part + jnp.where(z >= 2, got, 0.0)
    total = tie(total + got, feats[1])
    feats[2] = features_of(2, total)
    got = move(total, "y0")
    part = part + jnp.where(y % 2 == 1, got, 0.0)
    total = tie(total + got, feats[2])
    intra0 = local_of(0, total)
    got = move(total, "y1")
    part = tie(part + jnp.where(y >= 2, got, 0.0), intra0)
    intra1 = local_of(1, part)
    stack = jnp.concatenate([part, move(part, "x0")], axis=0)
    stack = tie(stack, intra1)
    feats[3], turned_grad, base = ready_of(stack)
    stack = jnp.concatenate([stack, move(stack, "x1")], axis=0)
    stack = tie(stack, feats[3])
    other = move(stack, "c")

    state, attended, dn, mine, *sends = call(
        main_kernel,
        [((ROWS, 128), BF16), ((GROUP, 4 * DIM), BF16), ((4 * DIM, GROUP), BF16)] + [((2 * PIECE, 128), F32)] * 4,
        [
            vmem((ROWS, 128)),
            vmem((DIM, 2 * ROWS), BF16),
            vmem((4 * DIM, GROUP)),
            vmem((ROWS, 128)),
            vmem((3, 2 * ROWS, GROUP), BF16),
            pltpu.SemaphoreType.DMA((3,)),
            vmem((ROWS, 128)),
            pltpu.SemaphoreType.DMA((1,)),
        ],
        [where, stack, other, base, second, turned_grad, intra0, intra1] + feats,
        specs=[SCALAR] + [WHOLE] * 3 + [LEFT] + [WHOLE] * 3 + [LEFT] * 3 + [WHOLE],
        limit=30,
    )

    qg_local, kv_a, kv_b = call(
        back_local_kernel,
        [((4 * DIM, GROUP), F32), ((GROUP // 2, 128), F32), ((GROUP // 2, 128), F32)],
        [vmem((4 * DIM, GROUP)), vmem((GROUP, 128))],
        [keys_values, queries, dn],
        limit=16,
    )
    own = mine + move(sends[0], 1) + move(sends[1], 2) + move(sends[2], 3)
    own = tie(own, kv_a)
    other_own = move(own, "c")
    chip = own + other_own
    core_grad = jnp.where(c == 0, other_own, 0.0)

    def state_part(j, dn, before):
        extra = [] if before is None else [before]
        return call(
            back_state_kernel,
            [((GROUP, 4 * DIM), BF16)],
            [vmem((4 * DIM, 256))] * 2 + [vmem((2 * ROWS, 256))] * 2 + [vmem((DIM, 128))] * 2,
            [queries, dn, state, qg_local] + extra,
            specs=[block((256, 256), (j, 0)), block((256, 256), (0, j)), WHOLE, block((256, 256), (0, j))]
            + [LEFT] * len(extra),
            out_specs=[block((256, 256), (j, 0))],
            grid=(1,),
            aliases={4: 0} if extra else None,
            limit=12,
        )[0]

    got = move(chip, "z0")
    got_a, got_b = move(kv_a, "x0"), move(kv_b, "x1")
    qg = state_part(0, tie(dn, chip), None)
    part = core_grad + jnp.where(z % 2 == 0, got, 0.0)
    total = tie(chip + got, qg)

    got = move(total, "z1")
    qg = state_part(1, tie(dn, total), qg)
    part = part + jnp.where(z < 2, got, 0.0)
    kv_a = tie(kv_a, qg) + got_a
    kv_b = tie(kv_b, qg) + got_b
    total = tie(total + got, qg, kv_a, kv_b)

    got = move(total, "y0")
    got_a, got_b = move(tie(kv_a, total), "x1"), move(tie(kv_b, total), "x0")
    qg = state_part(2, tie(dn, total), qg)
    part = part + jnp.where(y % 2 == 0, got, 0.0)
    total = tie(total + got, qg)

    got = move(total, "y1")
    qg = state_part(3, tie(dn, total, got_a, got_b), qg)
    part = tie(part + jnp.where(y < 2, got, 0.0), qg)
    every = total + got

    before, after = move(part, 1), move(part, 3)
    key_feats, turned_kv = call(
        key_feature_kernel,
        [((2 * ROWS, GROUP), BF16), ((128, GROUP), F32)],
        [],
        [keys_values, part],
        specs=[block((GROUP, 128), (0, 0)), block((8, 128), (0, 0))],
        out_specs=[block((2 * ROWS, GROUP), (0, 0)), block((128, GROUP), (0, 0))],
        grid=(1,),
        limit=12,
    )
    every_low, every_high = move(every[2 * PIECE - LOW :], 1), move(every[:HIGH], 3)
    before, after = tie(before, key_feats, every_low), tie(after, key_feats, every_high)
    across_a, across_b = move(after[:PIECE], 3), move(before[PIECE:], 1)

    (init_grad,) = call(
        total_kernel,
        [((DIM, FEATURES // 4), F32)],
        [vmem((ROWS, 128)), vmem((FEATURES, 128))],
        [where, every, every_low, every_high, first],
        specs=[SCALAR] + [WHOLE] * 4,
        limit=8,
    )
    across_a = tie(across_a, init_grad)
    (kv_grad,) = call(
        key_kernel,
        [((GROUP, 128), F32)],
        [vmem((ROWS, 128)), vmem((ROWS, 128), BF16), vmem((DIM, 2 * ROWS), BF16), vmem((128, GROUP))]
        + [vmem((2 * ROWS, 256))] * 2
        + [vmem((DIM, 128))] * 2,
        [where, part, before, after, across_a, across_b, second, turned_kv, kv_a, kv_b, got_a, got_b, key_feats],
        specs=[SCALAR] + [WHOLE] * 12,
        limit=20,
    )
    return attended, qg, kv_grad, init_grad


def solution(mesh):
    return jax.shard_map(
        per_device,
        mesh=mesh,
        in_specs=(P("seq", "head"), P("seq", None), P(), P("seq", "head")),
        out_specs=(P("seq", "head"), P("seq", "head"), P("seq", None), P(None, "head")),
        check_vma=False,
    )
```

```python
import functools

import jax
import jax.numpy as jnp
import numpy as np
from jax import lax
from jax.experimental import pallas as pl
from jax.experimental.pallas import tpu as pltpu
from jax.sharding import PartitionSpec as P

DIM = 64
GROUP = 1024
FEATURES = 2080
EPSILON = 1e-06
WIDTHS = [DIM - 8 * g for g in range(8)]
STARTS = [sum(4 * w for w in WIDTHS[:g]) for g in range(8)]
ROWS = sum(4 * w for w in WIDTHS)
PIECE = ROWS // 8
F32 = jnp.float32
BF16 = jnp.bfloat16
MIB = 1024 * 1024


DIAGONAL, BESIDE = 1.0 / np.sqrt(DIM), np.sqrt(2.0 / DIM)


def triu_start(a):
    return DIM * a - a * (a - 1) // 2


def dot(x, y):
    return lax.dot_general(x, y, (((1,), (0,)), ((), ())), preferred_element_type=F32)


def build_step(x_ref, base, phi_ref, lanes):
    for g in range(8):
        tail = x_ref[pl.ds(base + 8 * g, WIDTHS[g]), lanes]
        for half in range(2):
            parts = []
            for i in range(4):
                a = 8 * g + 4 * half + i
                parts.append(tail[a - 8 * g : a - 8 * g + 1, :] * tail)
            block = jnp.concatenate(parts, axis=0).astype(BF16)
            phi_ref[pl.ds(half * ROWS + STARTS[g], 4 * WIDTHS[g]), lanes] = block


def build_features(x_ref, base, phi_ref, tokens, start=0):
    def one(step, carry):
        build_step(x_ref, base, phi_ref, pl.ds(pl.multiple_of(start + step * 128, 128), 128))
        return carry

    lax.fori_loop(0, tokens // 128, one, 0)


def fold_step(x_ref, base, x_lane, d_ref, rows_ref, out_ref, out_base, at):
    lanes = pl.ds(at, 128)
    xl = pl.ds(x_lane + at, 128)
    x = x_ref[pl.ds(base, DIM), xl]
    acc = [jnp.zeros((8, 128), F32) for _ in range(8)]
    for g in range(8):
        for half in range(2):
            for i in range(4):
                a = 8 * g + 4 * half + i
                xa = x[a : a + 1, :]
                row = half * ROWS + STARTS[g] + i * WIDTHS[g]
                total = None
                for k in range(g, 8):
                    d = d_ref[pl.ds(row + 8 * (k - g), 8), lanes]
                    acc[k] = acc[k] + d * xa
                    term = d * x[8 * k : 8 * k + 8, :]
                    total = term if total is None else total + term
                rows_ref[a : a + 1, :] = jnp.sum(total, axis=0, keepdims=True)
    grad = jnp.concatenate(acc, axis=0) + rows_ref[...]
    out_ref[pl.ds(out_base, DIM), xl] = out_ref[pl.ds(out_base, DIM), xl] + grad


def low_lanes(shape):
    return lax.broadcasted_iota(jnp.int32, shape, 1) < 64


def update_kernel(kv_hbm, out_ref, x_ref, phi_ref, kv_ref, sems):
    fetch([(kv_hbm, kv_ref)], sems)[0].wait()
    kv = kv_ref[...]
    x_ref[...] = kv.astype(F32).T
    v = kv[:, DIM:]
    vv = jnp.concatenate([v, v], axis=1)
    low = low_lanes((ROWS, 128))
    for j in range(4):
        tokens = slice(256 * j, 256 * j + 256)
        for at in (256 * j, 256 * j + 128):
            build_step(x_ref, 0, phi_ref, pl.ds(at, 128))
        lo = dot(phi_ref[0:ROWS, tokens], vv[tokens])
        hi = dot(phi_ref[ROWS : 2 * ROWS, tokens], vv[tokens])
        part = jnp.where(low, lo, hi)
        out_ref[...] = part if j == 0 else out_ref[...] + part


def fetch(pairs, sems):
    copies = [pltpu.make_async_copy(a, b, sems.at[i]) for i, (a, b) in enumerate(pairs)]
    for copy in copies:
        copy.start()
    return copies


def init_kernel(init_hbm, out_ref, second_ref, t_ref, init_ref, sems):
    copy = fetch([(init_hbm, init_ref)], sems)[0]
    for g in range(8):
        shape = (WIDTHS[g], 128)
        row = lax.broadcasted_iota(jnp.int32, shape, 0)
        for i in range(4):
            own = jnp.where(low_lanes(shape), i, i + 4)
            squared = jnp.where(row == own, 1.0 / DIM, 2.0 / DIM)
            second_ref[pl.ds(STARTS[g] + i * WIDTHS[g], WIDTHS[g]), :] = jnp.where(row >= own, squared, 0.0)
    copy.wait()
    t_ref[...] = jnp.concatenate([init_ref[...], init_ref[...]], axis=0).T
    for g in range(8):
        shape = (WIDTHS[g], 128)
        row = lax.broadcasted_iota(jnp.int32, shape, 0)
        for i in range(4):
            rows = []
            for half in range(2):
                a = 8 * g + 4 * half + i
                rows.append(t_ref[pl.ds(triu_start(a) - (a - 8 * g), WIDTHS[g]), :])
            own = jnp.where(low_lanes(shape), i, i + 4)
            scaled = jnp.where(low_lanes(shape), rows[0], rows[1]) * jnp.where(row == own, DIAGONAL, BESIDE)
            out_ref[pl.ds(STARTS[g] + i * WIDTHS[g], WIDTHS[g]), :] = jnp.where(row >= own, scaled, 0.0)


def causal(rows, j):
    return lax.broadcasted_iota(jnp.int32, (rows, 256), 0) <= lax.broadcasted_iota(jnp.int32, (rows, 256), 1) + 256 * j


def local_kernel(kv_ref, q_ref, token_ref, out_ref, qt_ref):
    kv = kv_ref[...]
    k = kv[:, :DIM]
    vt = kv.astype(F32).T[DIM:].astype(BF16)
    qt_ref[...] = q_ref[...].astype(F32).T.astype(BF16)
    for hh in range(2):
        at = slice(hh * DIM, hh * DIM + DIM)
        for j in range(4):
            last = 256 * (j + 1)
            logits = dot(k[:last], qt_ref[at, 256 * j : last])
            w = jnp.where(causal(last, j), logits * logits * (1.0 / DIM), 0.0).astype(BF16)
            out_ref[at, 256 * j : last] = dot(vt[:, :last], w)


def ready_kernel(q_ref, g_ref, where_ref, before_ref, init_ref, second_ref, token_ref, out_ref, gt_out, base_out, x_ref):
    x_ref[...] = q_ref[...].astype(F32).T
    build_features(x_ref, DIM, out_ref, GROUP)
    gt_out[...] = g_ref[...].astype(F32).T
    core = where_ref[1].astype(F32)
    base_out[...] = init_ref[...] + second_ref[...] * (core * before_ref[...])


def key_feature_kernel(kv_ref, token_ref, out_ref, x_ref):
    x_ref[...] = kv_ref[...].astype(F32).T
    build_features(x_ref, 0, out_ref, GROUP)


def first_feature_kernel(q_hbm, token_ref, out_ref, x_ref, phi_ref, sems, q_ref, q_sems):
    fetch([(q_hbm.at[:, 0:128], q_ref)], q_sems)[0].wait()
    feature_kernel(0, q_ref, token_ref, out_ref, x_ref, phi_ref, sems)


def feature_kernel(hh, q_ref, token_ref, out_ref, x_ref, phi_ref, sems):
    x_ref[...] = q_ref[...].astype(F32).T
    copies = []
    for j in range(4):
        build_features(x_ref, DIM * hh, phi_ref, 256, 256 * j)
        lanes = pl.ds(256 * j, 256)
        copies.append(pltpu.make_async_copy(phi_ref.at[:, lanes], out_ref.at[:, lanes], sems.at[j]))
        copies[j].start()
    for copy in copies:
        copy.wait()


def sources(h):
    near = h + 1 - 2 * lax.rem(h, 2)
    return h, near, 3 - h, 3 - near


def place(where_ref, mine_ref, other_ref, out_ref):
    h, c = where_ref[0], where_ref[1]
    for s, source in enumerate(sources(h)):
        here = pl.ds(s * PIECE, PIECE)
        out_ref[pl.ds(pl.multiple_of((source * 2 + c) * PIECE, 8), PIECE), :] = mine_ref[here, :]
        out_ref[pl.ds(pl.multiple_of((source * 2 + 1 - c) * PIECE, 8), PIECE), :] = other_ref[here, :]


def flip_state(state, flat_ref):
    turned = state.T.astype(BF16)
    flat_ref[:, 0:ROWS] = turned[0:DIM]
    flat_ref[:, ROWS : 2 * ROWS] = turned[DIM : 2 * DIM]


def main_kernel(
    where_ref, mine_ref, other_ref, base_ref, second_ref, g_ref, intra0_ref, intra1_ref, f0, f1, f2, f3,
    state_out, att_out, dn_out, g0, g1, g2, g3,
    sum_ref, flat_ref, gt_ref, grad_ref, phi_ref, sems,
):
    copies = [pltpu.make_async_copy(f, phi_ref.at[i], sems.at[i]) for i, f in enumerate((f0, f1, f2))]
    copies[0].start()
    place(where_ref, mine_ref, other_ref, sum_ref)
    state = base_ref[...] + second_ref[...] * sum_ref[...]
    state_out[...] = state.astype(BF16)
    flip_state(state, flat_ref)
    order = (3, 0, 1, 2)
    copies[1].start()

    def features_of(step):
        return f3 if step == 0 else phi_ref.at[step - 1]

    def numer_of(step):
        hh = order[step]
        intra_ref = (intra0_ref, intra1_ref)[hh // 2]
        half = slice((hh % 2) * DIM, (hh % 2) * DIM + DIM)
        return dot(flat_ref[...], features_of(step)[...]) + intra_ref[half, :]

    following = numer_of(0)
    for step, hh in enumerate(order):
        at = slice(hh * DIM, hh * DIM + DIM)
        numer = following
        if step < 3:
            copies[step].wait()
            if step == 0:
                copies[2].start()
            following = numer_of(step + 1)
        scale = lax.rsqrt(jnp.mean(numer * numer, axis=0, keepdims=True) + EPSILON)
        y = numer * scale
        u = g_ref[at, :]
        dn = scale * (u - y * jnp.mean(u * y, axis=0, keepdims=True))
        gt_ref[at, :] = y
        dn_out[at, :] = dn.astype(BF16)
        twice = jnp.concatenate([dn, dn], axis=0).T.astype(BF16)
        feats = features_of(step)
        lo = dot(feats[0:ROWS], twice)
        hi = dot(feats[ROWS : 2 * ROWS], twice)
        total = jnp.where(low_lanes((ROWS, 128)), lo, hi)
        grad_ref[...] = total if step == 0 else grad_ref[...] + total
    for s, out in enumerate((g0, g1, g2, g3)):
        at = pl.multiple_of(lax.rem(where_ref[0] + s, 4) * 2 * PIECE, 8)
        out[...] = grad_ref[pl.ds(at, 2 * PIECE), :]
    att_out[...] = gt_ref[...].T.astype(BF16)


def back_local_kernel(kv_ref, q_ref, dn_ref, qg_out, kva_out, kvb_out, qt_ref, kvl_out):
    kv = kv_ref[...]
    k = kv[:, :DIM]
    v = kv[:, DIM:]
    kt = kv.astype(F32).T[:DIM].astype(BF16)
    qt_ref[...] = q_ref[...].astype(F32).T
    kvl_out[...] = jnp.zeros_like(kvl_out)
    low = low_lanes((256, 128))

    def head(hh, carry):
        at = pl.ds(pl.multiple_of(hh * DIM, DIM), DIM)
        for j in range(4):
            first, last = 256 * j, 256 * (j + 1)
            dnt = dn_ref[at, first:last]
            qt = qt_ref[at, first:last]
            logits = dot(k[:last], qt.astype(BF16))
            keep = causal(last, j)
            w = jnp.where(keep, logits * logits * (1.0 / DIM), 0.0).astype(BF16)
            dw = dot(v[:last], dnt)
            dl = jnp.where(keep, dw * logits * (2.0 / DIM), 0.0).astype(BF16)
            both = jnp.concatenate([qt, dnt.astype(F32)], axis=0).T.astype(BF16)
            qz = jnp.where(low, both, jnp.zeros_like(both))
            dnz = jnp.where(low, jnp.zeros_like(both), both)
            kvl_out[0:last, :] = kvl_out[0:last, :] + (dot(dl, qz) + dot(w, dnz))
            qg_out[at, first:last] = dot(kt[:, :last], dl)
        return carry

    lax.fori_loop(0, 4, head, 0)
    kva_out[...] = kvl_out[0 : GROUP // 2, :]
    kvb_out[...] = kvl_out[GROUP // 2 : GROUP, :]


def back_state_kernel(q_ref, dn_ref, state_ref, local_ref, *rest):
    out_ref, qt_ref, acc_ref, da_ref, db_ref, ra_ref, rb_ref = rest[-7:]
    qt_ref[...] = q_ref[...].astype(F32).T
    acc_ref[...] = local_ref[...]
    zeros = jnp.zeros((DIM, 256), BF16)

    def spread(hh, d_ref):
        dnt = dn_ref[hh * DIM : hh * DIM + DIM, :]
        d_ref[0:ROWS, :] = dot(state_ref[...], jnp.concatenate([dnt, zeros], axis=0))
        d_ref[ROWS : 2 * ROWS, :] = dot(state_ref[...], jnp.concatenate([zeros, dnt], axis=0))

    spread(0, da_ref)
    for hh in range(4):
        now, then = ((da_ref, db_ref), (db_ref, da_ref))[hh % 2]
        if hh < 3:
            spread(hh + 1, then)
        for step in range(2):
            fold_step(qt_ref, DIM * hh, 0, now, (ra_ref, rb_ref)[step], acc_ref, DIM * hh, 128 * step)
    out_ref[...] = acc_ref[...].T.astype(BF16)


def key_kernel(
    where_ref, part_ref, before_ref, after_ref, across_a_ref, across_b_ref, second_ref, x_ref,
    kv_a_ref, kv_b_ref, got_a_ref, got_b_ref, phi_ref,
    out_ref,
    sum_ref, low_ref, flat_ref, acc_ref, da_ref, db_ref, ra_ref, rb_ref,
):
    for s, refs in enumerate(((part_ref,), (after_ref,), (across_a_ref, across_b_ref), (before_ref,))):
        at = lax.rem(where_ref[0] + s, 4) * 2 * PIECE
        for i, ref in enumerate(refs):
            rows = 2 * PIECE // len(refs)
            sum_ref[pl.ds(pl.multiple_of(at + i * rows, 8), rows), :] = ref[...]
    state = second_ref[...] * sum_ref[...]
    low_ref[...] = state.astype(BF16)
    flip_state(state, flat_ref)
    acc_ref[0:DIM, :] = jnp.zeros((DIM, GROUP), F32)
    zeros = jnp.zeros((DIM, 256), BF16)

    def spread(j, d_ref):
        vt = x_ref[DIM : 2 * DIM, 256 * j : 256 * j + 256].astype(BF16)
        d_ref[0:ROWS, :] = dot(low_ref[...], jnp.concatenate([vt, zeros], axis=0))
        d_ref[ROWS : 2 * ROWS, :] = dot(low_ref[...], jnp.concatenate([zeros, vt], axis=0))

    spread(0, da_ref)
    for j in range(4):
        now, then = ((da_ref, db_ref), (db_ref, da_ref))[j % 2]
        if j < 3:
            spread(j + 1, then)
        else:
            acc_ref[DIM : 2 * DIM, :] = dot(flat_ref[...], phi_ref[...])
        for step in range(2):
            fold_step(x_ref, 0, 256 * j, now, (ra_ref, rb_ref)[step], acc_ref, 0, 128 * step)
    turned = acc_ref[...].T
    out_ref[0 : GROUP // 2, :] = (kv_a_ref[...] + got_a_ref[...]) + turned[0 : GROUP // 2]
    out_ref[GROUP // 2 : GROUP, :] = (kv_b_ref[...] + got_b_ref[...]) + turned[GROUP // 2 : GROUP]


LOW, HIGH = 96, 48


def total_kernel(where_ref, own_ref, low_ref, high_ref, out_ref, sum_ref, t_ref):
    width = FEATURES // 4
    for part in range(4):

        @pl.when(where_ref[0] == part)
        def _(part=part, first=part * width, last=(part + 1) * width):
            start = part * 2 * PIECE
            sum_ref[start : start + 2 * PIECE, :] = own_ref[...]
            if part > 0:
                sum_ref[start - LOW : start, :] = low_ref[...]
            if part < 3:
                sum_ref[start + 2 * PIECE : start + 2 * PIECE + HIGH, :] = high_ref[...]
            for a in reversed(range(DIM)):
                if triu_start(a) >= last or triu_start(a + 1) <= first:
                    continue
                g = a // 8
                at = pl.ds(STARTS[g] + (a % 4) * WIDTHS[g], WIDTHS[g])
                row = lax.broadcasted_iota(jnp.int32, (WIDTHS[g], 128), 0)
                piece = sum_ref[at, :] * jnp.where(row == a - 8 * g, DIAGONAL, BESIDE)
                if a % 8 >= 4:
                    piece = pltpu.roll(piece, 64, 1)
                t_ref[pl.ds(triu_start(a) - (a - 8 * g), WIDTHS[g]), :] = piece
            out_ref[...] = t_ref[first:last, :].T[0:DIM]


def vmem(shape, kind=F32):
    return pltpu.VMEM(shape, kind)


WHOLE = pl.BlockSpec(memory_space=pltpu.VMEM)
SCALAR = pl.BlockSpec(memory_space=pltpu.SMEM)
LEFT = pl.BlockSpec(memory_space=pltpu.HBM)


def block(shape, at):
    return pl.BlockSpec(shape, lambda i: at)


def call(kernel, outs, scratch, args, specs=None, out_specs=None, grid=(), aliases=None, limit=40):
    specs = specs or [WHOLE] * len(args)
    out_specs = out_specs or [WHOLE] * len(outs)
    args = [pltpu.with_memory_space_constraint(a, pltpu.HBM) if s is LEFT else a for a, s in zip(args, specs)]
    return pl.pallas_call(
        kernel,
        grid=grid,
        out_shape=[pltpu.HBM(s, k) if o is LEFT else jax.ShapeDtypeStruct(s, k) for (s, k), o in zip(outs, out_specs)],
        in_specs=specs,
        out_specs=out_specs,
        scratch_shapes=scratch,
        input_output_aliases=aliases or {},
        compiler_params=pltpu.CompilerParams(vmem_limit_bytes=limit * MIB),
    )(*args)


PAIRS = {
    "c": lambda x, y, z, c: (x, y, z, 1 - c),
    "z0": lambda x, y, z, c: (x, y, z ^ 1, c),
    "z1": lambda x, y, z, c: (x, y, 3 - z, c),
    "y0": lambda x, y, z, c: (x, y ^ 1, z, c),
    "y1": lambda x, y, z, c: (x, 3 - y, z, c),
}


def move(x, step):
    if step in PAIRS:
        pairs = []
        for j in range(32):
            _, y, z, c = PAIRS[step](0, j // 8, (j // 2) % 4, j % 2)
            pairs.append((j, y * 8 + z * 2 + c))
        return lax.ppermute(x, "seq", pairs)
    if step == "x0":
        return lax.ppermute(x, "head", [(j, j ^ 1) for j in range(4)])
    if step == "x1":
        return lax.ppermute(x, "head", [(j, 3 - j) for j in range(4)])
    return lax.ppermute(x, "head", [(j, (j + step) % 4) for j in range(4)])


def take(x, index, rows):
    return lax.dynamic_slice_in_dim(x, index * rows, rows, 0)


def tie(x, *others):
    return lax.optimization_barrier((x,) + others)[0]


def per_device(queries, keys_values, init_state, out_grad):
    h = lax.axis_index("head")
    seq = lax.axis_index("seq")
    c, z, y = seq % 2, (seq // 2) % 4, seq // 8
    where = jnp.stack([h, c]).astype(jnp.int32)
    half = h * 2 + c

    def features_of(hh, token):
        more = [vmem((GROUP, 128), BF16), pltpu.SemaphoreType.DMA((1,))] if hh == 0 else []
        return call(
            functools.partial(feature_kernel, hh % 2) if hh else first_feature_kernel,
            [((2 * ROWS, GROUP), BF16)],
            [vmem((128, GROUP)), vmem((2 * ROWS, GROUP), BF16), pltpu.SemaphoreType.DMA((4,))] + more,
            [queries, token],
            specs=[block((GROUP, 128), (0, hh // 2)) if hh else LEFT, block((8, 128), (0, 0))],
            out_specs=[LEFT],
            grid=(1,),
            limit=10,
        )[0]

    def ready_of(token):
        token_block = block((8, 128), (0, 0))
        shapes = [((2 * ROWS, GROUP), BF16), ((4 * DIM, GROUP), F32), ((ROWS, 128), F32)]
        return call(
            ready_kernel,
            shapes,
            [vmem((128, GROUP))],
            [queries, out_grad, where, other_update, init_low, second, token],
            specs=[block((GROUP, 128), (0, 1)), WHOLE, SCALAR, WHOLE, WHOLE, WHOLE, token_block],
            out_specs=[block(shape, (0, 0)) for shape, _ in shapes],
            grid=(1,),
            limit=16,
        )

    def local_of(p, token):
        return call(
            local_kernel,
            [((128, GROUP), F32)],
            [vmem((128, GROUP), BF16)],
            [keys_values, queries, token],
            specs=[WHOLE, block((GROUP, 128), (0, p)), block((8, 128), (0, 0))],
            out_specs=[block((128, GROUP), (0, 0))],
            grid=(1,),
            limit=10,
        )[0]

    (update,) = call(
        update_kernel,
        [((ROWS, 128), F32)],
        [
            vmem((128, GROUP)), vmem((2 * ROWS, GROUP), BF16), vmem((GROUP, 128), BF16), pltpu.SemaphoreType.DMA((1,)),
        ],
        [keys_values],
        specs=[LEFT],
        limit=12,
    )
    init_low, second = call(
        init_kernel,
        [((ROWS, 128), F32), ((ROWS, 128), F32)],
        [vmem((FEATURES, 128)), vmem((DIM, FEATURES)), pltpu.SemaphoreType.DMA((1,))],
        [tie(init_state, update)],
        specs=[LEFT],
        limit=8,
    )
    other_update = move(update, "c")
    chip = take(update, half, PIECE) + take(other_update, half, PIECE)
    chip = tie(chip, init_low)
    feats = [None] * 4
    feats[0] = features_of(0, chip)
    got = move(chip, "z0")
    part = jnp.where(z % 2 == 1, got, 0.0)
    total = tie(chip + got, feats[0])
    feats[1] = features_of(1, total)
    got = move(total, "z1")
    part = part + jnp.where(z >= 2, got, 0.0)
    total = tie(total + got, feats[1])
    feats[2] = features_of(2, total)
    got = move(total, "y0")
    part = part + jnp.where(y % 2 == 1, got, 0.0)
    total = tie(total + got, feats[2])
    intra0 = local_of(0, total)
    got = move(total, "y1")
    part = tie(part + jnp.where(y >= 2, got, 0.0), intra0)
    intra1 = local_of(1, part)
    stack = jnp.concatenate([part, move(part, "x0")], axis=0)
    stack = tie(stack, intra1)
    feats[3], turned_grad, base = ready_of(stack)
    stack = jnp.concatenate([stack, move(stack, "x1")], axis=0)
    stack = tie(stack, feats[3])
    other = move(stack, "c")

    state, attended, dn, mine, *sends = call(
        main_kernel,
        [((ROWS, 128), BF16), ((GROUP, 4 * DIM), BF16), ((4 * DIM, GROUP), BF16)] + [((2 * PIECE, 128), F32)] * 4,
        [
            vmem((ROWS, 128)),
            vmem((DIM, 2 * ROWS), BF16),
            vmem((4 * DIM, GROUP)),
            vmem((ROWS, 128)),
            vmem((3, 2 * ROWS, GROUP), BF16),
            pltpu.SemaphoreType.DMA((3,)),
        ],
        [where, stack, other, base, second, turned_grad, intra0, intra1] + feats,
        specs=[SCALAR] + [WHOLE] * 7 + [LEFT] * 3 + [WHOLE],
        limit=30,
    )

    qg_local, kv_a, kv_b = call(
        back_local_kernel,
        [((4 * DIM, GROUP), F32), ((GROUP // 2, 128), F32), ((GROUP // 2, 128), F32)],
        [vmem((4 * DIM, GROUP)), vmem((GROUP, 128))],
        [keys_values, queries, dn],
        limit=16,
    )
    own = mine + move(sends[0], 1) + move(sends[1], 2) + move(sends[2], 3)
    own = tie(own, kv_a)
    other_own = move(own, "c")
    chip = own + other_own
    core_grad = jnp.where(c == 0, other_own, 0.0)

    def state_part(j, dn, before):
        extra = [] if before is None else [before]
        return call(
            back_state_kernel,
            [((GROUP, 4 * DIM), BF16)],
            [vmem((4 * DIM, 256))] * 2 + [vmem((2 * ROWS, 256))] * 2 + [vmem((DIM, 128))] * 2,
            [queries, dn, state, qg_local] + extra,
            specs=[block((256, 256), (j, 0)), block((256, 256), (0, j)), WHOLE, block((256, 256), (0, j))]
            + [LEFT] * len(extra),
            out_specs=[block((256, 256), (j, 0))],
            grid=(1,),
            aliases={4: 0} if extra else None,
            limit=12,
        )[0]

    got = move(chip, "z0")
    got_a, got_b = move(kv_a, "x0"), move(kv_b, "x1")
    qg = state_part(0, tie(dn, chip), None)
    part = core_grad + jnp.where(z % 2 == 0, got, 0.0)
    total = tie(chip + got, qg)

    got = move(total, "z1")
    qg = state_part(1, tie(dn, total), qg)
    part = part + jnp.where(z < 2, got, 0.0)
    kv_a = tie(kv_a, qg) + got_a
    kv_b = tie(kv_b, qg) + got_b
    total = tie(total + got, qg, kv_a, kv_b)

    got = move(total, "y0")
    got_a, got_b = move(tie(kv_a, total), "x1"), move(tie(kv_b, total), "x0")
    qg = state_part(2, tie(dn, total), qg)
    part = part + jnp.where(y % 2 == 0, got, 0.0)
    total = tie(total + got, qg)

    got = move(total, "y1")
    qg = state_part(3, tie(dn, total, got_a, got_b), qg)
    part = tie(part + jnp.where(y < 2, got, 0.0), qg)
    every = total + got

    before, after = move(part, 1), move(part, 3)
    key_feats, turned_kv = call(
        key_feature_kernel,
        [((2 * ROWS, GROUP), BF16), ((128, GROUP), F32)],
        [],
        [keys_values, part],
        specs=[block((GROUP, 128), (0, 0)), block((8, 128), (0, 0))],
        out_specs=[block((2 * ROWS, GROUP), (0, 0)), block((128, GROUP), (0, 0))],
        grid=(1,),
        limit=12,
    )
    every_low, every_high = move(every[2 * PIECE - LOW :], 1), move(every[:HIGH], 3)
    before, after = tie(before, key_feats, every_low), tie(after, key_feats, every_high)
    across_a, across_b = move(after[:PIECE], 3), move(before[PIECE:], 1)

    (init_grad,) = call(
        total_kernel,
        [((DIM, FEATURES // 4), F32)],
        [vmem((ROWS, 128)), vmem((FEATURES, 128))],
        [where, every, every_low, every_high],
        specs=[SCALAR] + [WHOLE] * 3,
        limit=8,
    )
    across_a = tie(across_a, init_grad)
    (kv_grad,) = call(
        key_kernel,
        [((GROUP, 128), F32)],
        [vmem((ROWS, 128)), vmem((ROWS, 128), BF16), vmem((DIM, 2 * ROWS), BF16), vmem((128, GROUP))]
        + [vmem((2 * ROWS, 256))] * 2
        + [vmem((DIM, 128))] * 2,
        [where, part, before, after, across_a, across_b, second, turned_kv, kv_a, kv_b, got_a, got_b, key_feats],
        specs=[SCALAR] + [WHOLE] * 12,
        limit=20,
    )
    return attended, qg, kv_grad, init_grad


def solution(mesh):
    return jax.shard_map(
        per_device,
        mesh=mesh,
        in_specs=(P("seq", "head"), P("seq", None), P(), P("seq", "head")),
        out_specs=(P("seq", "head"), P("seq", "head"), P("seq", None), P(None, "head")),
        check_vma=False,
    )
```

```python
import functools

import jax
import jax.numpy as jnp
import numpy as np
from jax import lax
from jax.experimental import pallas as pl
from jax.experimental.pallas import tpu as pltpu
from jax.sharding import PartitionSpec as P

DIM = 64
GROUP = 1024
FEATURES = 2080
EPSILON = 1e-06
WIDTHS = [DIM - 8 * g for g in range(8)]
STARTS = [sum(4 * w for w in WIDTHS[:g]) for g in range(8)]
ROWS = sum(4 * w for w in WIDTHS)
PIECE = ROWS // 8
F32 = jnp.float32
BF16 = jnp.bfloat16
MIB = 1024 * 1024


DIAGONAL, BESIDE = 1.0 / np.sqrt(DIM), np.sqrt(2.0 / DIM)


def triu_start(a):
    return DIM * a - a * (a - 1) // 2


def dot(x, y):
    return lax.dot_general(x, y, (((1,), (0,)), ((), ())), preferred_element_type=F32)


def build_step(x_ref, base, phi_ref, lanes):
    for g in range(8):
        tail = x_ref[pl.ds(base + 8 * g, WIDTHS[g]), lanes]
        for half in range(2):
            parts = []
            for i in range(4):
                a = 8 * g + 4 * half + i
                parts.append(tail[a - 8 * g : a - 8 * g + 1, :] * tail)
            block = jnp.concatenate(parts, axis=0).astype(BF16)
            phi_ref[pl.ds(half * ROWS + STARTS[g], 4 * WIDTHS[g]), lanes] = block


def build_features(x_ref, base, phi_ref, tokens, start=0):
    def one(step, carry):
        build_step(x_ref, base, phi_ref, pl.ds(pl.multiple_of(start + step * 128, 128), 128))
        return carry

    lax.fori_loop(0, tokens // 128, one, 0)


def fold_step(x_ref, base, x_lane, d_ref, rows_ref, out_ref, out_base, at):
    lanes = pl.ds(at, 128)
    xl = pl.ds(x_lane + at, 128)
    x = x_ref[pl.ds(base, DIM), xl]
    acc = [jnp.zeros((8, 128), F32) for _ in range(8)]
    for g in range(8):
        for half in range(2):
            for i in range(4):
                a = 8 * g + 4 * half + i
                xa = x[a : a + 1, :]
                row = half * ROWS + STARTS[g] + i * WIDTHS[g]
                total = None
                for k in range(g, 8):
                    d = d_ref[pl.ds(row + 8 * (k - g), 8), lanes]
                    acc[k] = acc[k] + d * xa
                    term = d * x[8 * k : 8 * k + 8, :]
                    total = term if total is None else total + term
                rows_ref[a : a + 1, :] = jnp.sum(total, axis=0, keepdims=True)
    grad = jnp.concatenate(acc, axis=0) + rows_ref[...]
    out_ref[pl.ds(out_base, DIM), xl] = out_ref[pl.ds(out_base, DIM), xl] + grad


def low_lanes(shape):
    return lax.broadcasted_iota(jnp.int32, shape, 1) < 64


def update_kernel(kv_hbm, out_ref, x_ref, phi_ref, kv_ref, sems):
    fetch([(kv_hbm, kv_ref)], sems)[0].wait()
    kv = kv_ref[...]
    x_ref[...] = kv.astype(F32).T
    v = kv[:, DIM:]
    vv = jnp.concatenate([v, v], axis=1)
    low = low_lanes((ROWS, 128))
    for j in range(4):
        tokens = slice(256 * j, 256 * j + 256)
        for at in (256 * j, 256 * j + 128):
            build_step(x_ref, 0, phi_ref, pl.ds(at, 128))
        lo = dot(phi_ref[0:ROWS, tokens], vv[tokens])
        hi = dot(phi_ref[ROWS : 2 * ROWS, tokens], vv[tokens])
        part = jnp.where(low, lo, hi)
        out_ref[...] = part if j == 0 else out_ref[...] + part


def fetch(pairs, sems):
    copies = [pltpu.make_async_copy(a, b, sems.at[i]) for i, (a, b) in enumerate(pairs)]
    for copy in copies:
        copy.start()
    return copies


def init_kernel(init_hbm, out_ref, second_ref, t_ref, init_ref, sems):
    copy = fetch([(init_hbm, init_ref)], sems)[0]
    for g in range(8):
        shape = (WIDTHS[g], 128)
        row = lax.broadcasted_iota(jnp.int32, shape, 0)
        for i in range(4):
            own = jnp.where(low_lanes(shape), i, i + 4)
            squared = jnp.where(row == own, 1.0 / DIM, 2.0 / DIM)
            second_ref[pl.ds(STARTS[g] + i * WIDTHS[g], WIDTHS[g]), :] = jnp.where(row >= own, squared, 0.0)
    copy.wait()
    t_ref[...] = jnp.concatenate([init_ref[...], init_ref[...]], axis=0).T
    for g in range(8):
        shape = (WIDTHS[g], 128)
        row = lax.broadcasted_iota(jnp.int32, shape, 0)
        for i in range(4):
            rows = []
            for half in range(2):
                a = 8 * g + 4 * half + i
                rows.append(t_ref[pl.ds(triu_start(a) - (a - 8 * g), WIDTHS[g]), :])
            own = jnp.where(low_lanes(shape), i, i + 4)
            scaled = jnp.where(low_lanes(shape), rows[0], rows[1]) * jnp.where(row == own, DIAGONAL, BESIDE)
            out_ref[pl.ds(STARTS[g] + i * WIDTHS[g], WIDTHS[g]), :] = jnp.where(row >= own, scaled, 0.0)


def causal(rows, j):
    return lax.broadcasted_iota(jnp.int32, (rows, 256), 0) <= lax.broadcasted_iota(jnp.int32, (rows, 256), 1) + 256 * j


def local_kernel(kv_ref, q_ref, token_ref, out_ref, qt_ref):
    kv = kv_ref[...]
    k = kv[:, :DIM]
    vt = kv.astype(F32).T[DIM:].astype(BF16)
    qt_ref[...] = q_ref[...].astype(F32).T.astype(BF16)
    for hh in range(2):
        at = slice(hh * DIM, hh * DIM + DIM)
        for j in range(4):
            last = 256 * (j + 1)
            logits = dot(k[:last], qt_ref[at, 256 * j : last])
            w = jnp.where(causal(last, j), logits * logits * (1.0 / DIM), 0.0).astype(BF16)
            out_ref[at, 256 * j : last] = dot(vt[:, :last], w)


def ready_kernel(q_ref, g_ref, where_ref, before_ref, init_ref, second_ref, token_ref, out_ref, gt_out, base_out, x_ref):
    x_ref[...] = q_ref[...].astype(F32).T
    build_features(x_ref, DIM, out_ref, GROUP)
    gt_out[...] = g_ref[...].astype(F32).T
    core = where_ref[1].astype(F32)
    base_out[...] = init_ref[...] + second_ref[...] * (core * before_ref[...])


def key_feature_kernel(kv_ref, token_ref, out_ref, x_ref):
    x_ref[...] = kv_ref[...].astype(F32).T
    build_features(x_ref, 0, out_ref, GROUP)


def first_feature_kernel(q_hbm, token_ref, out_ref, x_ref, phi_ref, sems, q_ref, q_sems):
    fetch([(q_hbm.at[:, 0:128], q_ref)], q_sems)[0].wait()
    feature_kernel(0, q_ref, token_ref, out_ref, x_ref, phi_ref, sems)


def feature_kernel(hh, q_ref, token_ref, out_ref, x_ref, phi_ref, sems):
    x_ref[...] = q_ref[...].astype(F32).T
    copies = []
    for j in range(4):
        build_features(x_ref, DIM * hh, phi_ref, 256, 256 * j)
        lanes = pl.ds(256 * j, 256)
        copies.append(pltpu.make_async_copy(phi_ref.at[:, lanes], out_ref.at[:, lanes], sems.at[j]))
        copies[j].start()
    for copy in copies:
        copy.wait()


def sources(h):
    near = h + 1 - 2 * lax.rem(h, 2)
    return h, near, 3 - h, 3 - near


def place(where_ref, mine_ref, other_ref, out_ref):
    h, c = where_ref[0], where_ref[1]
    for s, source in enumerate(sources(h)):
        here = pl.ds(s * PIECE, PIECE)
        out_ref[pl.ds(pl.multiple_of((source * 2 + c) * PIECE, 8), PIECE), :] = mine_ref[here, :]
        out_ref[pl.ds(pl.multiple_of((source * 2 + 1 - c) * PIECE, 8), PIECE), :] = other_ref[here, :]


def flip_state(state, flat_ref):
    turned = state.T.astype(BF16)
    flat_ref[:, 0:ROWS] = turned[0:DIM]
    flat_ref[:, ROWS : 2 * ROWS] = turned[DIM : 2 * DIM]


def main_kernel(
    where_ref, mine_ref, other_ref, base_ref, second_ref, g_ref, intra0_ref, intra1_ref, f0, f1, f2, f3,
    state_out, att_out, dn_out, g0, g1, g2, g3,
    sum_ref, flat_ref, gt_ref, grad_ref, phi_ref, sems,
):
    copies = [pltpu.make_async_copy(f, phi_ref.at[i], sems.at[i]) for i, f in enumerate((f0, f1, f2))]
    copies[0].start()
    place(where_ref, mine_ref, other_ref, sum_ref)
    state = base_ref[...] + second_ref[...] * sum_ref[...]
    state_out[...] = state.astype(BF16)
    flip_state(state, flat_ref)
    order = (3, 0, 1, 2)
    copies[1].start()

    def features_of(step):
        return f3 if step == 0 else phi_ref.at[step - 1]

    def numer_of(step):
        hh = order[step]
        intra_ref = (intra0_ref, intra1_ref)[hh // 2]
        half = slice((hh % 2) * DIM, (hh % 2) * DIM + DIM)
        return dot(flat_ref[...], features_of(step)[...]) + intra_ref[half, :]

    following = numer_of(0)
    for step, hh in enumerate(order):
        at = slice(hh * DIM, hh * DIM + DIM)
        numer = following
        if step < 3:
            copies[step].wait()
            if step == 0:
                copies[2].start()
            following = numer_of(step + 1)
        scale = lax.rsqrt(jnp.mean(numer * numer, axis=0, keepdims=True) + EPSILON)
        y = numer * scale
        u = g_ref[at, :]
        dn = scale * (u - y * jnp.mean(u * y, axis=0, keepdims=True))
        gt_ref[at, :] = y
        dn_out[at, :] = dn.astype(BF16)
        twice = jnp.concatenate([dn, dn], axis=0).T.astype(BF16)
        feats = features_of(step)
        lo = dot(feats[0:ROWS], twice)
        hi = dot(feats[ROWS : 2 * ROWS], twice)
        total = jnp.where(low_lanes((ROWS, 128)), lo, hi)
        grad_ref[...] = total if step == 0 else grad_ref[...] + total
    for s, out in enumerate((g0, g1, g2, g3)):
        at = pl.multiple_of(lax.rem(where_ref[0] + s, 4) * 2 * PIECE, 8)
        out[...] = grad_ref[pl.ds(at, 2 * PIECE), :]
    att_out[...] = gt_ref[...].T.astype(BF16)


def back_local_kernel(kv_ref, q_ref, dn_ref, qg_out, kva_out, kvb_out, qt_ref, kvl_out):
    kv = kv_ref[...]
    k = kv[:, :DIM]
    v = kv[:, DIM:]
    kt = kv.astype(F32).T[:DIM].astype(BF16)
    qt_ref[...] = q_ref[...].astype(F32).T
    kvl_out[...] = jnp.zeros_like(kvl_out)
    low = low_lanes((256, 128))

    for hh in range(4):
        at = slice(hh * DIM, hh * DIM + DIM)
        for j in range(4):
            first, last = 256 * j, 256 * (j + 1)
            dnt = dn_ref[at, first:last]
            qt = qt_ref[at, first:last]
            logits = dot(k[:last], qt.astype(BF16))
            keep = causal(last, j)
            w = jnp.where(keep, logits * logits * (1.0 / DIM), 0.0).astype(BF16)
            dw = dot(v[:last], dnt)
            dl = jnp.where(keep, dw * logits * (2.0 / DIM), 0.0).astype(BF16)
            both = jnp.concatenate([qt, dnt.astype(F32)], axis=0).T.astype(BF16)
            qz = jnp.where(low, both, jnp.zeros_like(both))
            dnz = jnp.where(low, jnp.zeros_like(both), both)
            kvl_out[0:last, :] = kvl_out[0:last, :] + (dot(dl, qz) + dot(w, dnz))
            qg_out[at, first:last] = dot(kt[:, :last], dl)
    kva_out[...] = kvl_out[0 : GROUP // 2, :]
    kvb_out[...] = kvl_out[GROUP // 2 : GROUP, :]


def back_state_kernel(q_ref, dn_ref, state_ref, local_ref, *rest):
    out_ref, qt_ref, acc_ref, da_ref, db_ref, ra_ref, rb_ref = rest[-7:]
    qt_ref[...] = q_ref[...].astype(F32).T
    acc_ref[...] = local_ref[...]
    zeros = jnp.zeros((DIM, 256), BF16)

    def spread(hh, d_ref):
        dnt = dn_ref[hh * DIM : hh * DIM + DIM, :]
        d_ref[0:ROWS, :] = dot(state_ref[...], jnp.concatenate([dnt, zeros], axis=0))
        d_ref[ROWS : 2 * ROWS, :] = dot(state_ref[...], jnp.concatenate([zeros, dnt], axis=0))

    spread(0, da_ref)
    for hh in range(4):
        now, then = ((da_ref, db_ref), (db_ref, da_ref))[hh % 2]
        if hh < 3:
            spread(hh + 1, then)
        for step in range(2):
            fold_step(qt_ref, DIM * hh, 0, now, (ra_ref, rb_ref)[step], acc_ref, DIM * hh, 128 * step)
    out_ref[...] = acc_ref[...].T.astype(BF16)


def key_kernel(
    where_ref, part_ref, before_ref, after_ref, across_a_ref, across_b_ref, second_ref, x_ref,
    kv_a_ref, kv_b_ref, got_a_ref, got_b_ref, phi_ref,
    out_ref,
    sum_ref, low_ref, flat_ref, acc_ref, da_ref, db_ref, ra_ref, rb_ref,
):
    for s, refs in enumerate(((part_ref,), (after_ref,), (across_a_ref, across_b_ref), (before_ref,))):
        at = lax.rem(where_ref[0] + s, 4) * 2 * PIECE
        for i, ref in enumerate(refs):
            rows = 2 * PIECE // len(refs)
            sum_ref[pl.ds(pl.multiple_of(at + i * rows, 8), rows), :] = ref[...]
    state = second_ref[...] * sum_ref[...]
    low_ref[...] = state.astype(BF16)
    flip_state(state, flat_ref)
    acc_ref[0:DIM, :] = jnp.zeros((DIM, GROUP), F32)
    zeros = jnp.zeros((DIM, 256), BF16)

    def spread(j, d_ref):
        vt = x_ref[DIM : 2 * DIM, 256 * j : 256 * j + 256].astype(BF16)
        d_ref[0:ROWS, :] = dot(low_ref[...], jnp.concatenate([vt, zeros], axis=0))
        d_ref[ROWS : 2 * ROWS, :] = dot(low_ref[...], jnp.concatenate([zeros, vt], axis=0))

    spread(0, da_ref)
    for j in range(4):
        now, then = ((da_ref, db_ref), (db_ref, da_ref))[j % 2]
        if j < 3:
            spread(j + 1, then)
        else:
            acc_ref[DIM : 2 * DIM, :] = dot(flat_ref[...], phi_ref[...])
        for step in range(2):
            fold_step(x_ref, 0, 256 * j, now, (ra_ref, rb_ref)[step], acc_ref, 0, 128 * step)
    turned = acc_ref[...].T
    out_ref[0 : GROUP // 2, :] = (kv_a_ref[...] + got_a_ref[...]) + turned[0 : GROUP // 2]
    out_ref[GROUP // 2 : GROUP, :] = (kv_b_ref[...] + got_b_ref[...]) + turned[GROUP // 2 : GROUP]


LOW, HIGH = 96, 48


def total_kernel(where_ref, own_ref, low_ref, high_ref, out_ref, sum_ref, t_ref):
    width = FEATURES // 4
    for part in range(4):

        @pl.when(where_ref[0] == part)
        def _(part=part, first=part * width, last=(part + 1) * width):
            start = part * 2 * PIECE
            sum_ref[start : start + 2 * PIECE, :] = own_ref[...]
            if part > 0:
                sum_ref[start - LOW : start, :] = low_ref[...]
            if part < 3:
                sum_ref[start + 2 * PIECE : start + 2 * PIECE + HIGH, :] = high_ref[...]
            for a in reversed(range(DIM)):
                if triu_start(a) >= last or triu_start(a + 1) <= first:
                    continue
                g = a // 8
                at = pl.ds(STARTS[g] + (a % 4) * WIDTHS[g], WIDTHS[g])
                row = lax.broadcasted_iota(jnp.int32, (WIDTHS[g], 128), 0)
                piece = sum_ref[at, :] * jnp.where(row == a - 8 * g, DIAGONAL, BESIDE)
                if a % 8 >= 4:
                    piece = pltpu.roll(piece, 64, 1)
                t_ref[pl.ds(triu_start(a) - (a - 8 * g), WIDTHS[g]), :] = piece
            out_ref[...] = t_ref[first:last, :].T[0:DIM]


def vmem(shape, kind=F32):
    return pltpu.VMEM(shape, kind)


WHOLE = pl.BlockSpec(memory_space=pltpu.VMEM)
SCALAR = pl.BlockSpec(memory_space=pltpu.SMEM)
LEFT = pl.BlockSpec(memory_space=pltpu.HBM)


def block(shape, at):
    return pl.BlockSpec(shape, lambda i: at)


def call(kernel, outs, scratch, args, specs=None, out_specs=None, grid=(), aliases=None, limit=40):
    specs = specs or [WHOLE] * len(args)
    out_specs = out_specs or [WHOLE] * len(outs)
    args = [pltpu.with_memory_space_constraint(a, pltpu.HBM) if s is LEFT else a for a, s in zip(args, specs)]
    return pl.pallas_call(
        kernel,
        grid=grid,
        out_shape=[pltpu.HBM(s, k) if o is LEFT else jax.ShapeDtypeStruct(s, k) for (s, k), o in zip(outs, out_specs)],
        in_specs=specs,
        out_specs=out_specs,
        scratch_shapes=scratch,
        input_output_aliases=aliases or {},
        compiler_params=pltpu.CompilerParams(vmem_limit_bytes=limit * MIB),
    )(*args)


PAIRS = {
    "c": lambda x, y, z, c: (x, y, z, 1 - c),
    "z0": lambda x, y, z, c: (x, y, z ^ 1, c),
    "z1": lambda x, y, z, c: (x, y, 3 - z, c),
    "y0": lambda x, y, z, c: (x, y ^ 1, z, c),
    "y1": lambda x, y, z, c: (x, 3 - y, z, c),
}


def move(x, step):
    if step in PAIRS:
        pairs = []
        for j in range(32):
            _, y, z, c = PAIRS[step](0, j // 8, (j // 2) % 4, j % 2)
            pairs.append((j, y * 8 + z * 2 + c))
        return lax.ppermute(x, "seq", pairs)
    if step == "x0":
        return lax.ppermute(x, "head", [(j, j ^ 1) for j in range(4)])
    if step == "x1":
        return lax.ppermute(x, "head", [(j, 3 - j) for j in range(4)])
    return lax.ppermute(x, "head", [(j, (j + step) % 4) for j in range(4)])


def take(x, index, rows):
    return lax.dynamic_slice_in_dim(x, index * rows, rows, 0)


def tie(x, *others):
    return lax.optimization_barrier((x,) + others)[0]


def per_device(queries, keys_values, init_state, out_grad):
    h = lax.axis_index("head")
    seq = lax.axis_index("seq")
    c, z, y = seq % 2, (seq // 2) % 4, seq // 8
    where = jnp.stack([h, c]).astype(jnp.int32)
    half = h * 2 + c

    def features_of(hh, token):
        more = [vmem((GROUP, 128), BF16), pltpu.SemaphoreType.DMA((1,))] if hh == 0 else []
        return call(
            functools.partial(feature_kernel, hh % 2) if hh else first_feature_kernel,
            [((2 * ROWS, GROUP), BF16)],
            [vmem((128, GROUP)), vmem((2 * ROWS, GROUP), BF16), pltpu.SemaphoreType.DMA((4,))] + more,
            [queries, token],
            specs=[block((GROUP, 128), (0, hh // 2)) if hh else LEFT, block((8, 128), (0, 0))],
            out_specs=[LEFT],
            grid=(1,),
            limit=10,
        )[0]

    def ready_of(token):
        token_block = block((8, 128), (0, 0))
        shapes = [((2 * ROWS, GROUP), BF16), ((4 * DIM, GROUP), F32), ((ROWS, 128), F32)]
        return call(
            ready_kernel,
            shapes,
            [vmem((128, GROUP))],
            [queries, out_grad, where, other_update, init_low, second, token],
            specs=[block((GROUP, 128), (0, 1)), WHOLE, SCALAR, WHOLE, WHOLE, WHOLE, token_block],
            out_specs=[block(shape, (0, 0)) for shape, _ in shapes],
            grid=(1,),
            limit=16,
        )

    def local_of(p, token):
        return call(
            local_kernel,
            [((128, GROUP), F32)],
            [vmem((128, GROUP), BF16)],
            [keys_values, queries, token],
            specs=[WHOLE, block((GROUP, 128), (0, p)), block((8, 128), (0, 0))],
            out_specs=[block((128, GROUP), (0, 0))],
            grid=(1,),
            limit=10,
        )[0]

    (update,) = call(
        update_kernel,
        [((ROWS, 128), F32)],
        [
            vmem((128, GROUP)), vmem((2 * ROWS, GROUP), BF16), vmem((GROUP, 128), BF16), pltpu.SemaphoreType.DMA((1,)),
        ],
        [keys_values],
        specs=[LEFT],
        limit=12,
    )
    init_low, second = call(
        init_kernel,
        [((ROWS, 128), F32), ((ROWS, 128), F32)],
        [vmem((FEATURES, 128)), vmem((DIM, FEATURES)), pltpu.SemaphoreType.DMA((1,))],
        [tie(init_state, update)],
        specs=[LEFT],
        limit=8,
    )
    other_update = move(update, "c")
    chip = take(update, half, PIECE) + take(other_update, half, PIECE)
    chip = tie(chip, init_low)
    feats = [None] * 4
    feats[0] = features_of(0, chip)
    got = move(chip, "z0")
    part = jnp.where(z % 2 == 1, got, 0.0)
    total = tie(chip + got, feats[0])
    feats[1] = features_of(1, total)
    got = move(total, "z1")
    part = part + jnp.where(z >= 2, got, 0.0)
    total = tie(total + got, feats[1])
    feats[2] = features_of(2, total)
    got = move(total, "y0")
    part = part + jnp.where(y % 2 == 1, got, 0.0)
    total = tie(total + got, feats[2])
    intra0 = local_of(0, total)
    got = move(total, "y1")
    part = tie(part + jnp.where(y >= 2, got, 0.0), intra0)
    intra1 = local_of(1, part)
    stack = jnp.concatenate([part, move(part, "x0")], axis=0)
    stack = tie(stack, intra1)
    feats[3], turned_grad, base = ready_of(stack)
    stack = jnp.concatenate([stack, move(stack, "x1")], axis=0)
    stack = tie(stack, feats[3])
    other = move(stack, "c")

    state, attended, dn, mine, *sends = call(
        main_kernel,
        [((ROWS, 128), BF16), ((GROUP, 4 * DIM), BF16), ((4 * DIM, GROUP), BF16)] + [((2 * PIECE, 128), F32)] * 4,
        [
            vmem((ROWS, 128)),
            vmem((DIM, 2 * ROWS), BF16),
            vmem((4 * DIM, GROUP)),
            vmem((ROWS, 128)),
            vmem((3, 2 * ROWS, GROUP), BF16),
            pltpu.SemaphoreType.DMA((3,)),
        ],
        [where, stack, other, base, second, turned_grad, intra0, intra1] + feats,
        specs=[SCALAR] + [WHOLE] * 7 + [LEFT] * 3 + [WHOLE],
        limit=30,
    )

    qg_local, kv_a, kv_b = call(
        back_local_kernel,
        [((4 * DIM, GROUP), F32), ((GROUP // 2, 128), F32), ((GROUP // 2, 128), F32)],
        [vmem((4 * DIM, GROUP)), vmem((GROUP, 128))],
        [keys_values, queries, dn],
        limit=16,
    )
    own = mine + move(sends[0], 1) + move(sends[1], 2) + move(sends[2], 3)
    own = tie(own, kv_a)
    other_own = move(own, "c")
    chip = own + other_own
    core_grad = jnp.where(c == 0, other_own, 0.0)

    def state_part(j, dn, before):
        extra = [] if before is None else [before]
        return call(
            back_state_kernel,
            [((GROUP, 4 * DIM), BF16)],
            [vmem((4 * DIM, 256))] * 2 + [vmem((2 * ROWS, 256))] * 2 + [vmem((DIM, 128))] * 2,
            [queries, dn, state, qg_local] + extra,
            specs=[block((256, 256), (j, 0)), block((256, 256), (0, j)), WHOLE, block((256, 256), (0, j))]
            + [LEFT] * len(extra),
            out_specs=[block((256, 256), (j, 0))],
            grid=(1,),
            aliases={4: 0} if extra else None,
            limit=12,
        )[0]

    got = move(chip, "z0")
    got_a, got_b = move(kv_a, "x0"), move(kv_b, "x1")
    qg = state_part(0, tie(dn, chip), None)
    part = core_grad + jnp.where(z % 2 == 0, got, 0.0)
    total = tie(chip + got, qg)

    got = move(total, "z1")
    qg = state_part(1, tie(dn, total), qg)
    part = part + jnp.where(z < 2, got, 0.0)
    kv_a = tie(kv_a, qg) + got_a
    kv_b = tie(kv_b, qg) + got_b
    total = tie(total + got, qg, kv_a, kv_b)

    got = move(total, "y0")
    got_a, got_b = move(tie(kv_a, total), "x1"), move(tie(kv_b, total), "x0")
    qg = state_part(2, tie(dn, total), qg)
    part = part + jnp.where(y % 2 == 0, got, 0.0)
    total = tie(total + got, qg)

    got = move(total, "y1")
    qg = state_part(3, tie(dn, total, got_a, got_b), qg)
    part = tie(part + jnp.where(y < 2, got, 0.0), qg)
    every = total + got

    before, after = move(part, 1), move(part, 3)
    key_feats, turned_kv = call(
        key_feature_kernel,
        [((2 * ROWS, GROUP), BF16), ((128, GROUP), F32)],
        [],
        [keys_values, part],
        specs=[block((GROUP, 128), (0, 0)), block((8, 128), (0, 0))],
        out_specs=[block((2 * ROWS, GROUP), (0, 0)), block((128, GROUP), (0, 0))],
        grid=(1,),
        limit=12,
    )
    every_low, every_high = move(every[2 * PIECE - LOW :], 1), move(every[:HIGH], 3)
    before, after = tie(before, key_feats, every_low), tie(after, key_feats, every_high)
    across_a, across_b = move(after[:PIECE], 3), move(before[PIECE:], 1)

    (init_grad,) = call(
        total_kernel,
        [((DIM, FEATURES // 4), F32)],
        [vmem((ROWS, 128)), vmem((FEATURES, 128))],
        [where, every, every_low, every_high],
        specs=[SCALAR] + [WHOLE] * 3,
        limit=8,
    )
    across_a = tie(across_a, init_grad)
    (kv_grad,) = call(
        key_kernel,
        [((GROUP, 128), F32)],
        [vmem((ROWS, 128)), vmem((ROWS, 128), BF16), vmem((DIM, 2 * ROWS), BF16), vmem((128, GROUP))]
        + [vmem((2 * ROWS, 256))] * 2
        + [vmem((DIM, 128))] * 2,
        [where, part, before, after, across_a, across_b, second, turned_kv, kv_a, kv_b, got_a, got_b, key_feats],
        specs=[SCALAR] + [WHOLE] * 12,
        limit=20,
    )
    return attended, qg, kv_grad, init_grad


def solution(mesh):
    return jax.shard_map(
        per_device,
        mesh=mesh,
        in_specs=(P("seq", "head"), P("seq", None), P(), P("seq", "head")),
        out_specs=(P("seq", "head"), P("seq", "head"), P("seq", None), P(None, "head")),
        check_vma=False,
    )
```

```python
import functools

import jax
import jax.numpy as jnp
import numpy as np
from jax import lax
from jax.experimental import pallas as pl
from jax.experimental.pallas import tpu as pltpu
from jax.sharding import PartitionSpec as P

DIM = 64
GROUP = 1024
FEATURES = 2080
EPSILON = 1e-06
WIDTHS = [DIM - 8 * g for g in range(8)]
STARTS = [sum(4 * w for w in WIDTHS[:g]) for g in range(8)]
ROWS = sum(4 * w for w in WIDTHS)
PIECE = ROWS // 8
F32 = jnp.float32
BF16 = jnp.bfloat16
MIB = 1024 * 1024


DIAGONAL, BESIDE = 1.0 / np.sqrt(DIM), np.sqrt(2.0 / DIM)


def triu_start(a):
    return DIM * a - a * (a - 1) // 2


def dot(x, y):
    return lax.dot_general(x, y, (((1,), (0,)), ((), ())), preferred_element_type=F32)


def build_step(x_ref, base, phi_ref, lanes):
    for g in range(8):
        tail = x_ref[pl.ds(base + 8 * g, WIDTHS[g]), lanes]
        for half in range(2):
            parts = []
            for i in range(4):
                a = 8 * g + 4 * half + i
                parts.append(tail[a - 8 * g : a - 8 * g + 1, :] * tail)
            block = jnp.concatenate(parts, axis=0).astype(BF16)
            phi_ref[pl.ds(half * ROWS + STARTS[g], 4 * WIDTHS[g]), lanes] = block


def build_features(x_ref, base, phi_ref, tokens, start=0):
    def one(step, carry):
        build_step(x_ref, base, phi_ref, pl.ds(pl.multiple_of(start + step * 128, 128), 128))
        return carry

    lax.fori_loop(0, tokens // 128, one, 0)


def fold_step(x_ref, base, x_lane, d_ref, rows_ref, out_ref, out_base, at):
    lanes = pl.ds(at, 128)
    xl = pl.ds(x_lane + at, 128)
    x = x_ref[pl.ds(base, DIM), xl]
    acc = [jnp.zeros((8, 128), F32) for _ in range(8)]
    for g in range(8):
        for half in range(2):
            for i in range(4):
                a = 8 * g + 4 * half + i
                xa = x[a : a + 1, :]
                row = half * ROWS + STARTS[g] + i * WIDTHS[g]
                total = None
                for k in range(g, 8):
                    d = d_ref[pl.ds(row + 8 * (k - g), 8), lanes]
                    acc[k] = acc[k] + d * xa
                    term = d * x[8 * k : 8 * k + 8, :]
                    total = term if total is None else total + term
                rows_ref[a : a + 1, :] = jnp.sum(total, axis=0, keepdims=True)
    grad = jnp.concatenate(acc, axis=0) + rows_ref[...]
    out_ref[pl.ds(out_base, DIM), xl] = out_ref[pl.ds(out_base, DIM), xl] + grad


def low_lanes(shape):
    return lax.broadcasted_iota(jnp.int32, shape, 1) < 64


def update_kernel(kv_hbm, out_ref, x_ref, phi_ref, kv_ref, sems):
    fetch([(kv_hbm, kv_ref)], sems)[0].wait()
    kv = kv_ref[...]
    x_ref[...] = kv.astype(F32).T
    v = kv[:, DIM:]
    vv = jnp.concatenate([v, v], axis=1)
    low = low_lanes((ROWS, 128))
    for j in range(4):
        tokens = slice(256 * j, 256 * j + 256)
        for at in (256 * j, 256 * j + 128):
            build_step(x_ref, 0, phi_ref, pl.ds(at, 128))
        lo = dot(phi_ref[0:ROWS, tokens], vv[tokens])
        hi = dot(phi_ref[ROWS : 2 * ROWS, tokens], vv[tokens])
        part = jnp.where(low, lo, hi)
        out_ref[...] = part if j == 0 else out_ref[...] + part


def fetch(pairs, sems):
    copies = [pltpu.make_async_copy(a, b, sems.at[i]) for i, (a, b) in enumerate(pairs)]
    for copy in copies:
        copy.start()
    return copies


def init_kernel(init_hbm, out_ref, second_ref, t_ref, init_ref, sems):
    copy = fetch([(init_hbm, init_ref)], sems)[0]
    for g in range(8):
        shape = (WIDTHS[g], 128)
        row = lax.broadcasted_iota(jnp.int32, shape, 0)
        for i in range(4):
            own = jnp.where(low_lanes(shape), i, i + 4)
            squared = jnp.where(row == own, 1.0 / DIM, 2.0 / DIM)
            second_ref[pl.ds(STARTS[g] + i * WIDTHS[g], WIDTHS[g]), :] = jnp.where(row >= own, squared, 0.0)
    copy.wait()
    t_ref[...] = jnp.concatenate([init_ref[...], init_ref[...]], axis=0).T
    for g in range(8):
        shape = (WIDTHS[g], 128)
        row = lax.broadcasted_iota(jnp.int32, shape, 0)
        for i in range(4):
            rows = []
            for half in range(2):
                a = 8 * g + 4 * half + i
                rows.append(t_ref[pl.ds(triu_start(a) - (a - 8 * g), WIDTHS[g]), :])
            own = jnp.where(low_lanes(shape), i, i + 4)
            scaled = jnp.where(low_lanes(shape), rows[0], rows[1]) * jnp.where(row == own, DIAGONAL, BESIDE)
            out_ref[pl.ds(STARTS[g] + i * WIDTHS[g], WIDTHS[g]), :] = jnp.where(row >= own, scaled, 0.0)


def causal(rows, j):
    return lax.broadcasted_iota(jnp.int32, (rows, 256), 0) <= lax.broadcasted_iota(jnp.int32, (rows, 256), 1) + 256 * j


def local_kernel(kv_ref, q_ref, token_ref, out_ref, qt_ref):
    kv = kv_ref[...]
    k = kv[:, :DIM]
    vt = kv.astype(F32).T[DIM:].astype(BF16)
    qt_ref[...] = q_ref[...].astype(F32).T.astype(BF16)
    for hh in range(2):
        at = slice(hh * DIM, hh * DIM + DIM)
        for j in range(4):
            last = 256 * (j + 1)
            logits = dot(k[:last], qt_ref[at, 256 * j : last])
            w = jnp.where(causal(last, j), logits * logits * (1.0 / DIM), 0.0).astype(BF16)
            out_ref[at, 256 * j : last] = dot(vt[:, :last], w)


def ready_kernel(q_ref, g_ref, where_ref, before_ref, init_ref, second_ref, token_ref, out_ref, gt_out, base_out, x_ref):
    x_ref[...] = q_ref[...].astype(F32).T
    build_features(x_ref, DIM, out_ref, GROUP)
    gt_out[...] = g_ref[...].astype(F32).T
    core = where_ref[1].astype(F32)
    base_out[...] = init_ref[...] + second_ref[...] * (core * before_ref[...])


def key_feature_kernel(kv_ref, token_ref, out_ref, x_ref):
    x_ref[...] = kv_ref[...].astype(F32).T
    build_features(x_ref, 0, out_ref, GROUP)


def first_feature_kernel(q_hbm, token_ref, out_ref, x_ref, phi_ref, sems, q_ref, q_sems):
    fetch([(q_hbm.at[:, 0:128], q_ref)], q_sems)[0].wait()
    feature_kernel(0, q_ref, token_ref, out_ref, x_ref, phi_ref, sems)


def feature_kernel(hh, q_ref, token_ref, out_ref, x_ref, phi_ref, sems):
    x_ref[...] = q_ref[...].astype(F32).T
    copies = []
    for j in range(4):
        build_features(x_ref, DIM * hh, phi_ref, 256, 256 * j)
        lanes = pl.ds(256 * j, 256)
        copies.append(pltpu.make_async_copy(phi_ref.at[:, lanes], out_ref.at[:, lanes], sems.at[j]))
        copies[j].start()
    for copy in copies:
        copy.wait()


def sources(h):
    near = h + 1 - 2 * lax.rem(h, 2)
    return h, near, 3 - h, 3 - near


def place(where_ref, mine_ref, other_ref, out_ref):
    h, c = where_ref[0], where_ref[1]
    for s, source in enumerate(sources(h)):
        here = pl.ds(s * PIECE, PIECE)
        out_ref[pl.ds(pl.multiple_of((source * 2 + c) * PIECE, 8), PIECE), :] = mine_ref[here, :]
        out_ref[pl.ds(pl.multiple_of((source * 2 + 1 - c) * PIECE, 8), PIECE), :] = other_ref[here, :]


def flip_state(state, flat_ref):
    turned = state.T.astype(BF16)
    flat_ref[:, 0:ROWS] = turned[0:DIM]
    flat_ref[:, ROWS : 2 * ROWS] = turned[DIM : 2 * DIM]


def main_kernel(
    where_ref, mine_ref, other_ref, base_ref, second_ref, g_ref, intra0_ref, intra1_ref, f0, f1, f2, f3,
    state_out, att_out, dn_out, g0, g1, g2, g3,
    sum_ref, flat_ref, gt_ref, grad_ref, phi_ref, sems,
):
    copies = [pltpu.make_async_copy(f, phi_ref.at[i], sems.at[i]) for i, f in enumerate((f0, f1, f2))]
    copies[0].start()
    h, c = where_ref[0], where_ref[1]
    for s, source in enumerate(sources(h)):
        here = pl.ds(s * PIECE, PIECE)
        for ref, core in ((mine_ref, c), (other_ref, 1 - c)):
            at = pl.ds(pl.multiple_of((source * 2 + core) * PIECE, 8), PIECE)
            sum_ref[at, :] = base_ref[at, :] + second_ref[at, :] * ref[here, :]
    state = sum_ref[...]
    state_out[...] = state.astype(BF16)
    flip_state(state, flat_ref)
    order = (3, 0, 1, 2)
    copies[1].start()

    def features_of(step):
        return f3 if step == 0 else phi_ref.at[step - 1]

    def numer_of(step):
        hh = order[step]
        intra_ref = (intra0_ref, intra1_ref)[hh // 2]
        half = slice((hh % 2) * DIM, (hh % 2) * DIM + DIM)
        return dot(flat_ref[...], features_of(step)[...]) + intra_ref[half, :]

    following = numer_of(0)
    for step, hh in enumerate(order):
        at = slice(hh * DIM, hh * DIM + DIM)
        numer = following
        if step < 3:
            copies[step].wait()
            if step == 0:
                copies[2].start()
            following = numer_of(step + 1)
        scale = lax.rsqrt(jnp.mean(numer * numer, axis=0, keepdims=True) + EPSILON)
        y = numer * scale
        u = g_ref[at, :]
        dn = scale * (u - y * jnp.mean(u * y, axis=0, keepdims=True))
        gt_ref[at, :] = y
        dn_out[at, :] = dn.astype(BF16)
        twice = jnp.concatenate([dn, dn], axis=0).T.astype(BF16)
        feats = features_of(step)
        lo = dot(feats[0:ROWS], twice)
        hi = dot(feats[ROWS : 2 * ROWS], twice)
        total = jnp.where(low_lanes((ROWS, 128)), lo, hi)
        grad_ref[...] = total if step == 0 else grad_ref[...] + total
    for s, out in enumerate((g0, g1, g2, g3)):
        at = pl.multiple_of(lax.rem(where_ref[0] + s, 4) * 2 * PIECE, 8)
        out[...] = grad_ref[pl.ds(at, 2 * PIECE), :]
    att_out[...] = gt_ref[...].T.astype(BF16)


def back_local_kernel(kv_ref, q_ref, dn_ref, qg_out, kva_out, kvb_out, qt_ref, kvl_out):
    kv = kv_ref[...]
    k = kv[:, :DIM]
    v = kv[:, DIM:]
    kt = kv.astype(F32).T[:DIM].astype(BF16)
    qt_ref[...] = q_ref[...].astype(F32).T
    kvl_out[...] = jnp.zeros_like(kvl_out)
    low = low_lanes((256, 128))

    for hh in range(4):
        at = slice(hh * DIM, hh * DIM + DIM)
        for j in range(4):
            first, last = 256 * j, 256 * (j + 1)
            dnt = dn_ref[at, first:last]
            qt = qt_ref[at, first:last]
            logits = dot(k[:last], qt.astype(BF16))
            keep = causal(last, j)
            w = jnp.where(keep, logits * logits * (1.0 / DIM), 0.0).astype(BF16)
            dw = dot(v[:last], dnt)
            dl = jnp.where(keep, dw * logits * (2.0 / DIM), 0.0).astype(BF16)
            both = jnp.concatenate([qt, dnt.astype(F32)], axis=0).T.astype(BF16)
            qz = jnp.where(low, both, jnp.zeros_like(both))
            dnz = jnp.where(low, jnp.zeros_like(both), both)
            kvl_out[0:last, :] = kvl_out[0:last, :] + (dot(dl, qz) + dot(w, dnz))
            qg_out[at, first:last] = dot(kt[:, :last], dl)
    kva_out[...] = kvl_out[0 : GROUP // 2, :]
    kvb_out[...] = kvl_out[GROUP // 2 : GROUP, :]


def back_state_kernel(q_ref, dn_ref, state_ref, local_ref, *rest):
    out_ref, qt_ref, acc_ref, da_ref, db_ref, ra_ref, rb_ref = rest[-7:]
    qt_ref[...] = q_ref[...].astype(F32).T
    acc_ref[...] = local_ref[...]
    zeros = jnp.zeros((DIM, 256), BF16)

    def spread(hh, d_ref):
        dnt = dn_ref[hh * DIM : hh * DIM + DIM, :]
        d_ref[0:ROWS, :] = dot(state_ref[...], jnp.concatenate([dnt, zeros], axis=0))
        d_ref[ROWS : 2 * ROWS, :] = dot(state_ref[...], jnp.concatenate([zeros, dnt], axis=0))

    spread(0, da_ref)
    for hh in range(4):
        now, then = ((da_ref, db_ref), (db_ref, da_ref))[hh % 2]
        if hh < 3:
            spread(hh + 1, then)
        for step in range(2):
            fold_step(qt_ref, DIM * hh, 0, now, (ra_ref, rb_ref)[step], acc_ref, DIM * hh, 128 * step)
    out_ref[...] = acc_ref[...].T.astype(BF16)


def key_kernel(
    where_ref, part_ref, before_ref, after_ref, across_a_ref, across_b_ref, second_ref, x_ref,
    kv_a_ref, kv_b_ref, got_a_ref, got_b_ref, phi_ref,
    out_ref,
    sum_ref, low_ref, flat_ref, acc_ref, da_ref, db_ref, ra_ref, rb_ref,
):
    for s, refs in enumerate(((part_ref,), (after_ref,), (across_a_ref, across_b_ref), (before_ref,))):
        at = lax.rem(where_ref[0] + s, 4) * 2 * PIECE
        for i, ref in enumerate(refs):
            rows = 2 * PIECE // len(refs)
            sum_ref[pl.ds(pl.multiple_of(at + i * rows, 8), rows), :] = ref[...]
    state = second_ref[...] * sum_ref[...]
    low_ref[...] = state.astype(BF16)
    flip_state(state, flat_ref)
    acc_ref[0:DIM, :] = jnp.zeros((DIM, GROUP), F32)
    zeros = jnp.zeros((DIM, 256), BF16)

    def spread(j, d_ref):
        vt = x_ref[DIM : 2 * DIM, 256 * j : 256 * j + 256].astype(BF16)
        d_ref[0:ROWS, :] = dot(low_ref[...], jnp.concatenate([vt, zeros], axis=0))
        d_ref[ROWS : 2 * ROWS, :] = dot(low_ref[...], jnp.concatenate([zeros, vt], axis=0))

    spread(0, da_ref)
    for j in range(4):
        now, then = ((da_ref, db_ref), (db_ref, da_ref))[j % 2]
        if j < 3:
            spread(j + 1, then)
        else:
            acc_ref[DIM : 2 * DIM, :] = dot(flat_ref[...], phi_ref[...])
        for step in range(2):
            fold_step(x_ref, 0, 256 * j, now, (ra_ref, rb_ref)[step], acc_ref, 0, 128 * step)
    turned = acc_ref[...].T
    out_ref[0 : GROUP // 2, :] = (kv_a_ref[...] + got_a_ref[...]) + turned[0 : GROUP // 2]
    out_ref[GROUP // 2 : GROUP, :] = (kv_b_ref[...] + got_b_ref[...]) + turned[GROUP // 2 : GROUP]


LOW, HIGH = 96, 48


def total_kernel(where_ref, own_ref, low_ref, high_ref, out_ref, sum_ref, t_ref):
    width = FEATURES // 4
    for part in range(4):

        @pl.when(where_ref[0] == part)
        def _(part=part, first=part * width, last=(part + 1) * width):
            start = part * 2 * PIECE
            sum_ref[start : start + 2 * PIECE, :] = own_ref[...]
            if part > 0:
                sum_ref[start - LOW : start, :] = low_ref[...]
            if part < 3:
                sum_ref[start + 2 * PIECE : start + 2 * PIECE + HIGH, :] = high_ref[...]
            for a in reversed(range(DIM)):
                if triu_start(a) >= last or triu_start(a + 1) <= first:
                    continue
                g = a // 8
                at = pl.ds(STARTS[g] + (a % 4) * WIDTHS[g], WIDTHS[g])
                row = lax.broadcasted_iota(jnp.int32, (WIDTHS[g], 128), 0)
                piece = sum_ref[at, :] * jnp.where(row == a - 8 * g, DIAGONAL, BESIDE)
                if a % 8 >= 4:
                    piece = pltpu.roll(piece, 64, 1)
                t_ref[pl.ds(triu_start(a) - (a - 8 * g), WIDTHS[g]), :] = piece
            out_ref[...] = t_ref[first:last, :].T[0:DIM]


def vmem(shape, kind=F32):
    return pltpu.VMEM(shape, kind)


WHOLE = pl.BlockSpec(memory_space=pltpu.VMEM)
SCALAR = pl.BlockSpec(memory_space=pltpu.SMEM)
LEFT = pl.BlockSpec(memory_space=pltpu.HBM)


def block(shape, at):
    return pl.BlockSpec(shape, lambda i: at)


def call(kernel, outs, scratch, args, specs=None, out_specs=None, grid=(), aliases=None, limit=40):
    specs = specs or [WHOLE] * len(args)
    out_specs = out_specs or [WHOLE] * len(outs)
    args = [pltpu.with_memory_space_constraint(a, pltpu.HBM) if s is LEFT else a for a, s in zip(args, specs)]
    return pl.pallas_call(
        kernel,
        grid=grid,
        out_shape=[pltpu.HBM(s, k) if o is LEFT else jax.ShapeDtypeStruct(s, k) for (s, k), o in zip(outs, out_specs)],
        in_specs=specs,
        out_specs=out_specs,
        scratch_shapes=scratch,
        input_output_aliases=aliases or {},
        compiler_params=pltpu.CompilerParams(vmem_limit_bytes=limit * MIB),
    )(*args)


PAIRS = {
    "c": lambda x, y, z, c: (x, y, z, 1 - c),
    "z0": lambda x, y, z, c: (x, y, z ^ 1, c),
    "z1": lambda x, y, z, c: (x, y, 3 - z, c),
    "y0": lambda x, y, z, c: (x, y ^ 1, z, c),
    "y1": lambda x, y, z, c: (x, 3 - y, z, c),
}


def move(x, step):
    if step in PAIRS:
        pairs = []
        for j in range(32):
            _, y, z, c = PAIRS[step](0, j // 8, (j // 2) % 4, j % 2)
            pairs.append((j, y * 8 + z * 2 + c))
        return lax.ppermute(x, "seq", pairs)
    if step == "x0":
        return lax.ppermute(x, "head", [(j, j ^ 1) for j in range(4)])
    if step == "x1":
        return lax.ppermute(x, "head", [(j, 3 - j) for j in range(4)])
    return lax.ppermute(x, "head", [(j, (j + step) % 4) for j in range(4)])


def take(x, index, rows):
    return lax.dynamic_slice_in_dim(x, index * rows, rows, 0)


def tie(x, *others):
    return lax.optimization_barrier((x,) + others)[0]


def per_device(queries, keys_values, init_state, out_grad):
    h = lax.axis_index("head")
    seq = lax.axis_index("seq")
    c, z, y = seq % 2, (seq // 2) % 4, seq // 8
    where = jnp.stack([h, c]).astype(jnp.int32)
    half = h * 2 + c

    def features_of(hh, token):
        more = [vmem((GROUP, 128), BF16), pltpu.SemaphoreType.DMA((1,))] if hh == 0 else []
        return call(
            functools.partial(feature_kernel, hh % 2) if hh else first_feature_kernel,
            [((2 * ROWS, GROUP), BF16)],
            [vmem((128, GROUP)), vmem((2 * ROWS, GROUP), BF16), pltpu.SemaphoreType.DMA((4,))] + more,
            [queries, token],
            specs=[block((GROUP, 128), (0, hh // 2)) if hh else LEFT, block((8, 128), (0, 0))],
            out_specs=[LEFT],
            grid=(1,),
            limit=10,
        )[0]

    def ready_of(token):
        token_block = block((8, 128), (0, 0))
        shapes = [((2 * ROWS, GROUP), BF16), ((4 * DIM, GROUP), F32), ((ROWS, 128), F32)]
        return call(
            ready_kernel,
            shapes,
            [vmem((128, GROUP))],
            [queries, out_grad, where, other_update, init_low, second, token],
            specs=[block((GROUP, 128), (0, 1)), WHOLE, SCALAR, WHOLE, WHOLE, WHOLE, token_block],
            out_specs=[block(shape, (0, 0)) for shape, _ in shapes],
            grid=(1,),
            limit=16,
        )

    def local_of(p, token):
        return call(
            local_kernel,
            [((128, GROUP), F32)],
            [vmem((128, GROUP), BF16)],
            [keys_values, queries, token],
            specs=[WHOLE, block((GROUP, 128), (0, p)), block((8, 128), (0, 0))],
            out_specs=[block((128, GROUP), (0, 0))],
            grid=(1,),
            limit=10,
        )[0]

    (update,) = call(
        update_kernel,
        [((ROWS, 128), F32)],
        [
            vmem((128, GROUP)), vmem((2 * ROWS, GROUP), BF16), vmem((GROUP, 128), BF16), pltpu.SemaphoreType.DMA((1,)),
        ],
        [keys_values],
        specs=[LEFT],
        limit=12,
    )
    init_low, second = call(
        init_kernel,
        [((ROWS, 128), F32), ((ROWS, 128), F32)],
        [vmem((FEATURES, 128)), vmem((DIM, FEATURES)), pltpu.SemaphoreType.DMA((1,))],
        [tie(init_state, update)],
        specs=[LEFT],
        limit=8,
    )
    other_update = move(update, "c")
    chip = take(update, half, PIECE) + take(other_update, half, PIECE)
    chip = tie(chip, init_low)
    feats = [None] * 4
    feats[0] = features_of(0, chip)
    got = move(chip, "z0")
    part = jnp.where(z % 2 == 1, got, 0.0)
    total = tie(chip + got, feats[0])
    feats[1] = features_of(1, total)
    got = move(total, "z1")
    part = part + jnp.where(z >= 2, got, 0.0)
    total = tie(total + got, feats[1])
    feats[2] = features_of(2, total)
    got = move(total, "y0")
    part = part + jnp.where(y % 2 == 1, got, 0.0)
    total = tie(total + got, feats[2])
    intra0 = local_of(0, total)
    got = move(total, "y1")
    part = tie(part + jnp.where(y >= 2, got, 0.0), intra0)
    intra1 = local_of(1, part)
    stack = jnp.concatenate([part, move(part, "x0")], axis=0)
    stack = tie(stack, intra1)
    feats[3], turned_grad, base = ready_of(stack)
    stack = jnp.concatenate([stack, move(stack, "x1")], axis=0)
    stack = tie(stack, feats[3])
    other = move(stack, "c")

    state, attended, dn, mine, *sends = call(
        main_kernel,
        [((ROWS, 128), BF16), ((GROUP, 4 * DIM), BF16), ((4 * DIM, GROUP), BF16)] + [((2 * PIECE, 128), F32)] * 4,
        [
            vmem((ROWS, 128)),
            vmem((DIM, 2 * ROWS), BF16),
            vmem((4 * DIM, GROUP)),
            vmem((ROWS, 128)),
            vmem((3, 2 * ROWS, GROUP), BF16),
            pltpu.SemaphoreType.DMA((3,)),
        ],
        [where, stack, other, base, second, turned_grad, intra0, intra1] + feats,
        specs=[SCALAR] + [WHOLE] * 7 + [LEFT] * 3 + [WHOLE],
        limit=30,
    )

    qg_local, kv_a, kv_b = call(
        back_local_kernel,
        [((4 * DIM, GROUP), F32), ((GROUP // 2, 128), F32), ((GROUP // 2, 128), F32)],
        [vmem((4 * DIM, GROUP)), vmem((GROUP, 128))],
        [keys_values, queries, dn],
        limit=16,
    )
    own = mine + move(sends[0], 1) + move(sends[1], 2) + move(sends[2], 3)
    own = tie(own, kv_a)
    other_own = move(own, "c")
    chip = own + other_own
    core_grad = jnp.where(c == 0, other_own, 0.0)

    def state_part(j, dn, before):
        extra = [] if before is None else [before]
        return call(
            back_state_kernel,
            [((GROUP, 4 * DIM), BF16)],
            [vmem((4 * DIM, 256))] * 2 + [vmem((2 * ROWS, 256))] * 2 + [vmem((DIM, 128))] * 2,
            [queries, dn, state, qg_local] + extra,
            specs=[block((256, 256), (j, 0)), block((256, 256), (0, j)), WHOLE, block((256, 256), (0, j))]
            + [LEFT] * len(extra),
            out_specs=[block((256, 256), (j, 0))],
            grid=(1,),
            aliases={4: 0} if extra else None,
            limit=12,
        )[0]

    got = move(chip, "z0")
    got_a, got_b = move(kv_a, "x0"), move(kv_b, "x1")
    qg = state_part(0, tie(dn, chip), None)
    part = core_grad + jnp.where(z % 2 == 0, got, 0.0)
    total = tie(chip + got, qg)

    got = move(total, "z1")
    qg = state_part(1, tie(dn, total), qg)
    part = part + jnp.where(z < 2, got, 0.0)
    kv_a = tie(kv_a, qg) + got_a
    kv_b = tie(kv_b, qg) + got_b
    total = tie(total + got, qg, kv_a, kv_b)

    got = move(total, "y0")
    got_a, got_b = move(tie(kv_a, total), "x1"), move(tie(kv_b, total), "x0")
    qg = state_part(2, tie(dn, total), qg)
    part = part + jnp.where(y % 2 == 0, got, 0.0)
    total = tie(total + got, qg)

    got = move(total, "y1")
    qg = state_part(3, tie(dn, total), qg)
    part = tie(part + jnp.where(y < 2, got, 0.0), qg)
    every = total + got

    before, after = move(part, 1), move(part, 3)
    key_feats, turned_kv = call(
        key_feature_kernel,
        [((2 * ROWS, GROUP), BF16), ((128, GROUP), F32)],
        [],
        [keys_values, tie(part, got_a, got_b)],
        specs=[block((GROUP, 128), (0, 0)), block((8, 128), (0, 0))],
        out_specs=[block((2 * ROWS, GROUP), (0, 0)), block((128, GROUP), (0, 0))],
        grid=(1,),
        limit=12,
    )
    every_low, every_high = move(every[2 * PIECE - LOW :], 1), move(every[:HIGH], 3)
    before, after = tie(before, key_feats, every_low), tie(after, key_feats, every_high)
    across_a, across_b = move(after[:PIECE], 3), move(before[PIECE:], 1)

    (init_grad,) = call(
        total_kernel,
        [((DIM, FEATURES // 4), F32)],
        [vmem((ROWS, 128)), vmem((FEATURES, 128))],
        [where, every, every_low, every_high],
        specs=[SCALAR] + [WHOLE] * 3,
        limit=8,
    )
    across_a = tie(across_a, init_grad)
    (kv_grad,) = call(
        key_kernel,
        [((GROUP, 128), F32)],
        [vmem((ROWS, 128)), vmem((ROWS, 128), BF16), vmem((DIM, 2 * ROWS), BF16), vmem((128, GROUP))]
        + [vmem((2 * ROWS, 256))] * 2
        + [vmem((DIM, 128))] * 2,
        [where, part, before, after, across_a, across_b, second, turned_kv, kv_a, kv_b, got_a, got_b, key_feats],
        specs=[SCALAR] + [WHOLE] * 12,
        limit=20,
    )
    return attended, qg, kv_grad, init_grad


def solution(mesh):
    return jax.shard_map(
        per_device,
        mesh=mesh,
        in_specs=(P("seq", "head"), P("seq", None), P(), P("seq", "head")),
        out_specs=(P("seq", "head"), P("seq", "head"), P("seq", None), P(None, "head")),
        check_vma=False,
    )
```
